512 devices in a mesh: doc: 16 (over z, core), ctx: 32 (over y, x).
Axes of the slice: x: 4, y: 8, z: 8, core: 2. Of those that a mesh axis runs over, the one named last changes fastest.
Arguments:
- tokens: bfloat16 [65536, 3584], P(('doc', 'ctx')), parts along dimension 0, may hold values from -6 to 6
- queries: bfloat16 [65536, 1792], P(('doc', 'ctx')), parts along dimension 0, may hold values from -320 to 320
- key_matrix: bfloat16 [3584, 256], P('ctx'), may hold values from -0.09375 to 0.09375
- value_matrix: bfloat16 [3584, 256], P('ctx'), may hold values from -0.09375 to 0.09375
- doc_tiles: int32 [32], P('doc'), parts along dimension 0, may hold values from 1 to 6, 8 in all
- question_lengths: int32 [32], P('doc'), parts along dimension 0, may hold values from 1 to 16, as said below
Outputs:
- attended: bfloat16 [65536, 1792], P(('doc', 'ctx')), parts along dimension 0
The draws below stay inside these ranges and needn't reach their ends.
There are 16 independent parts, one for each index of `doc`. The reference program is written for one: setup_inputs(seed, part) draws one part's arguments, and reference() takes and returns one part's arrays. A program takes and returns all parts, laid end to end along the dimension named above; an argument that names none is the same for every part. Nothing has to cross between parts.
Inputs may be any that keep to these rules, and one draw needn't show every extreme that they name: `doc_tiles`: document lengths in tiles of 512 tokens; they sum to 8 and the longest has at most 6 tiles. `question_lengths`: some document has exactly 16 question tokens.
All inputs are finite; a program needn't handle non-finite values.
Results may differ from the reference program's by a relative error of at most 0.012.
The reference program's roundings to bfloat16 on the way count: a program that leaves them out, or rounds other values in their place, can miss the bound.
Values may be sent and summed in bfloat16 or wider, within the bound.
No kernel may reach another device: no remote copies, remote signals or barrier semaphores. Data moves between devices by JAX's collectives and lax.ppermute only.
A program may use at most 64 MiB of HBM per device.

```python
import math
import jax
import jax.numpy as jnp
import numpy as np
from jax import lax

MODEL_WIDTH = 3584
HEAD_SIZE = 128
QUERY_HEADS = 14
KEY_VALUE_HEADS = 2
WINDOW_REACH = 512
TILE_TOKENS = 512
QUESTION_LIMIT = 16
TOKEN_SLOTS = 4096
TILES = 8
NDOC = 2
MAXT = 6


def draw_tokens(key, part):
    key = jax.random.fold_in(key, 11)
    key_base = jax.random.fold_in(key, 0)
    base = jax.random.normal(key_base, (TOKEN_SLOTS, MODEL_WIDTH), jnp.float32)
    return jnp.clip(base, -6.0, 6.0).astype(jnp.bfloat16)


def draw_queries(key, part):
    key = jax.random.fold_in(key, 23)
    key_base = jax.random.fold_in(key, 0)
    base = jax.random.normal(key_base, (TOKEN_SLOTS, QUERY_HEADS * HEAD_SIZE), jnp.float32)
    return jnp.clip(base, -320.0, 320.0).astype(jnp.bfloat16)


def draw_question_lengths(key, part):
    key = jax.random.fold_in(key, 37)
    key_count, key_full = jax.random.split(key)
    counts = jax.random.randint(key_count, (NDOC,), 1, QUESTION_LIMIT + 1)
    full_doc = jax.random.randint(key_full, (), 0, NDOC)
    return jnp.where(jnp.arange(NDOC) == full_doc, QUESTION_LIMIT, counts).astype(jnp.int32)


def level_of(stream_key, shape, cuts, low, high):
    gain, own = 1.0, jax.random.fold_in(stream_key, 6)
    for dim, shards_of in cuts:
        draws = jnp.exp(jax.random.uniform(jax.random.fold_in(own, dim), (shards_of,), jnp.float32, low / len(cuts), high / len(cuts)))
        gain = gain * jnp.repeat(draws, shape[dim] // shards_of).reshape([-1 if axis == dim else 1 for axis in range(len(shape))])
    return gain


def profile(number_of, total, bound, slope):
    portions = [(1 << 20) // math.isqrt(rank ** slope) + 1 for rank in range(2, number_of + 1)]
    rest, given = total - bound - (number_of - 1), [1] * (number_of - 1)
    while rest > 0:
        free = [i for i in range(number_of - 1) if given[i] < bound]
        pool, remaining = sum([portions[i] for i in free]), rest
        for i in free:
            more = min(bound - given[i], max(1, remaining * portions[i] // pool), rest)
            given[i] = given[i] + more
            rest = rest - more
    return np.array([bound] + given)


def ragged_sizes(own_key, amount, total, reach, lean):
    if amount == 2:
        one = jax.random.randint(own_key, (), max(1, total - reach), min(reach, total - 1) + 1)
        return jnp.stack([one, total - one])
    tallies = jnp.asarray(profile(amount, total, reach, lean), jnp.int32)
    twos = (amount - 1) // 2
    giver, sink = tallies[1:1 + 2 * twos:2], tallies[2:2 + 2 * twos:2]
    margin = jnp.minimum(giver - 1, reach - sink)
    passed = jax.random.randint(jax.random.fold_in(own_key, 1), (twos,), 0, 1 << 20) % (margin + 1)
    tallies = tallies.at[1:1 + 2 * twos:2].set(giver - passed).at[2:2 + 2 * twos:2].set(sink + passed)
    return tallies[jax.random.permutation(jax.random.fold_in(own_key, 2), amount)]


def noise(stream_key, extent, deviation, limit, cuts=(), kind=jnp.bfloat16):
    array = deviation * jax.random.normal(stream_key, extent, jnp.float32)
    if cuts:
        array = array * level_of(stream_key, extent, cuts, -0.22, 0.18)
    return jnp.clip(array, -limit, limit).astype(kind)


def setup_inputs(seed: int = 0, part: int = 0) -> dict:
    arg_keys = jax.random.split(jax.random.key(seed), 7)
    part_splits = jax.random.split(jax.random.fold_in(arg_keys[6], part), 7)
    return {
        "tokens": draw_tokens(jax.random.fold_in(jax.random.fold_in(arg_keys[6], part), 71), part),
        "queries": draw_queries(jax.random.fold_in(jax.random.fold_in(arg_keys[6], part), 71), part),
        "key_matrix": noise(arg_keys[2], (MODEL_WIDTH, KEY_VALUE_HEADS * HEAD_SIZE), MODEL_WIDTH ** -0.5, 0.09375, ((0, 32),)),
        "value_matrix": noise(arg_keys[3], (MODEL_WIDTH, KEY_VALUE_HEADS * HEAD_SIZE), MODEL_WIDTH ** -0.5, 0.09375, ((0, 32),)),
        "doc_tiles": ragged_sizes(part_splits[4], NDOC, TILES, MAXT, 1).astype(jnp.int32),
        "question_lengths": draw_question_lengths(jax.random.fold_in(jax.random.fold_in(arg_keys[6], part), 71), part),
    }


masked_score = -1e+30

def bounds(doc_tiles):
    doc_ends = (jnp.cumsum(doc_tiles.astype(jnp.int32)) * TILE_TOKENS).astype(jnp.int32)
    starts = (doc_ends - doc_tiles.astype(jnp.int32) * TILE_TOKENS).astype(jnp.int32)
    return (starts, doc_ends)

def reference(tokens, queries, key_matrix, value_matrix, doc_tiles, question_lengths):
    query_group_count = QUERY_HEADS // KEY_VALUE_HEADS
    scaling = 1.0 / math.sqrt(HEAD_SIZE)
    highest = lax.Precision.HIGHEST
    every_key_row = jnp.dot(tokens, key_matrix, preferred_element_type=jnp.float32).astype(jnp.bfloat16)
    value_rows = jnp.dot(tokens, value_matrix, preferred_element_type=jnp.float32).astype(jnp.bfloat16)
    starts, doc_ends = bounds(doc_tiles)
    lengths = question_lengths.astype(jnp.int32)
    padded_keys = jnp.pad(every_key_row, ((WINDOW_REACH, WINDOW_REACH), (0, 0)))
    padded_values = jnp.pad(value_rows, ((WINDOW_REACH, WINDOW_REACH), (0, 0)))

    def tile_band(tile_index):
        first_row_index = (tile_index * TILE_TOKENS).astype(jnp.int32)
        doc_index = (jnp.sum((starts <= first_row_index).astype(jnp.int32)) - 1).astype(jnp.int32)
        document_start = starts[doc_index]
        doc_last = doc_ends[doc_index]
        question_count = lengths[doc_index]
        query_tile_rows = lax.dynamic_slice_in_dim(queries, first_row_index, TILE_TOKENS, 0).astype(jnp.float32).reshape(TILE_TOKENS, KEY_VALUE_HEADS, query_group_count, HEAD_SIZE)
        window_keys = lax.dynamic_slice_in_dim(padded_keys, first_row_index, TILE_TOKENS + 2 * WINDOW_REACH, 0).astype(jnp.float32).reshape(TILE_TOKENS + 2 * WINDOW_REACH, KEY_VALUE_HEADS, HEAD_SIZE)
        window_values = lax.dynamic_slice_in_dim(padded_values, first_row_index, TILE_TOKENS + 2 * WINDOW_REACH, 0).astype(jnp.float32).reshape(TILE_TOKENS + 2 * WINDOW_REACH, KEY_VALUE_HEADS, HEAD_SIZE)
        distant_keys = lax.dynamic_slice_in_dim(every_key_row, document_start, QUESTION_LIMIT, 0).astype(jnp.float32).reshape(QUESTION_LIMIT, KEY_VALUE_HEADS, HEAD_SIZE)
        distant_values = lax.dynamic_slice_in_dim(value_rows, document_start, QUESTION_LIMIT, 0).astype(jnp.float32).reshape(QUESTION_LIMIT, KEY_VALUE_HEADS, HEAD_SIZE)
        query_pos = first_row_index + jnp.arange(TILE_TOKENS, dtype=jnp.int32)
        key_pos = first_row_index - WINDOW_REACH + jnp.arange(TILE_TOKENS + 2 * WINDOW_REACH, dtype=jnp.int32)
        near_valid = (jnp.abs(key_pos[None, :] - query_pos[:, None]) <= WINDOW_REACH) & (key_pos >= document_start + question_count)[None, :] & (key_pos < doc_last)[None, :]
        far_valid = jnp.arange(QUESTION_LIMIT, dtype=jnp.int32) < question_count
        near_scores = jnp.einsum('tkgd,nkd->kgtn', query_tile_rows, window_keys, precision=highest) * scaling
        far_scores = jnp.einsum('tkgd,nkd->kgtn', query_tile_rows, distant_keys, precision=highest) * scaling
        near_scores = jnp.where(near_valid, near_scores, masked_score)
        far_scores = jnp.where(far_valid, far_scores, masked_score)
        peak = jnp.maximum(near_scores.max(-1), far_scores.max(-1))
        near_probs = jnp.exp(near_scores - peak[..., None])
        far_probs = jnp.exp(far_scores - peak[..., None])
        totals = near_probs.sum(-1) + far_probs.sum(-1)
        near_round = lax.optimization_barrier(near_probs.astype(jnp.bfloat16)).astype(jnp.float32)
        far_round = lax.optimization_barrier(far_probs.astype(jnp.bfloat16)).astype(jnp.float32)
        output = jnp.einsum('kgtn,nkd->tkgd', near_round, window_values, precision=highest)
        output = output + jnp.einsum('kgtn,nkd->tkgd', far_round, distant_values, precision=highest)
        output = output / jnp.transpose(totals, (2, 0, 1))[..., None]
        return output.reshape(TILE_TOKENS, QUERY_HEADS * HEAD_SIZE)
    flattened_keys = every_key_row.astype(jnp.float32).reshape(TOKEN_SLOTS, KEY_VALUE_HEADS, HEAD_SIZE)
    flattened_values = value_rows.astype(jnp.float32).reshape(TOKEN_SLOTS, KEY_VALUE_HEADS, HEAD_SIZE)

    def ask_doc(doc_index):
        document_start = starts[doc_index]
        doc_last = doc_ends[doc_index]
        query_tile_rows = lax.dynamic_slice_in_dim(queries, document_start, QUESTION_LIMIT, 0).astype(jnp.float32).reshape(QUESTION_LIMIT, KEY_VALUE_HEADS, query_group_count, HEAD_SIZE)
        scores = jnp.einsum('qkgd,nkd->qkgn', query_tile_rows, flattened_keys, precision=highest) * scaling
        positions = jnp.arange(TOKEN_SLOTS, dtype=jnp.int32)
        valid_keys = (positions >= document_start) & (positions < doc_last)
        scores = jnp.where(valid_keys, scores, masked_score)
        peak = scores.max(-1)
        probs = jnp.exp(scores - peak[..., None])
        totals = probs.sum(-1)
        output = jnp.einsum('qkgn,nkd->qkgd', probs, flattened_values, precision=highest) / totals[..., None]
        return output.reshape(QUESTION_LIMIT, QUERY_HEADS * HEAD_SIZE)
    asked_rows = lax.map(ask_doc, jnp.arange(NDOC, dtype=jnp.int32))
    banded = lax.map(tile_band, jnp.arange(TILES, dtype=jnp.int32)).reshape(TOKEN_SLOTS, QUERY_HEADS * HEAD_SIZE)

    def place_doc(doc_index, result):
        document_start = starts[doc_index]
        current = lax.dynamic_slice_in_dim(result, document_start, QUESTION_LIMIT, 0)
        keep_rows = (jnp.arange(QUESTION_LIMIT, dtype=jnp.int32) < lengths[doc_index])[:, None]
        return lax.dynamic_update_slice_in_dim(result, jnp.where(keep_rows, asked_rows[doc_index], current), document_start, 0)
    result = lax.fori_loop(0, NDOC, place_doc, banded)
    return result.astype(jnp.bfloat16)
```

```python
import functools
import math

import jax
import jax.numpy as jnp
from jax import lax
from jax.experimental import pallas as pl
from jax.experimental.pallas import tpu as pltpu
from jax.sharding import Mesh, PartitionSpec as P

HEAD = 128
TILE = 512
ASK = 16
GROUP = 7
KV = 2
ROWS = 128
XS = 4
YS = 8
PACK = KV * GROUP * ASK + 16
SCALE = 1.0 / math.sqrt(HEAD)
MASKED = -1e30
NT = (((1,), (1,)), ((), ()))
bf16, f32 = jnp.bfloat16, jnp.float32

Y, X, CORE, START, STOP, ASKED = range(6)


def spec(space):
    return pl.BlockSpec(memory_space=space)


def call(body, out, ins, scratch=(), flops=0, moved=0):
    return pl.pallas_call(
        body,
        out_shape=out,
        in_specs=[spec(pltpu.SMEM)] + [spec(pltpu.VMEM)] * (ins - 1),
        out_specs=spec(pltpu.VMEM),
        scratch_shapes=list(scratch),
        compiler_params=pltpu.CompilerParams(vmem_limit_bytes=24 * 1024 * 1024),
        cost_estimate=pl.CostEstimate(flops=flops, bytes_accessed=moved, transcendentals=0),
    )


def project_body(ids, weights, mine, theirs, out, whole):
    depth = weights.shape[2]
    for x in range(XS):
        for y in range(YS):
            whole[pl.ds((XS * y + x) * depth, depth), :] = weights[x, y]
    core = ids[CORE]
    for part, tokens in ((core, mine), (1 - core, theirs)):
        rows = jnp.dot(tokens[...], whole[...], preferred_element_type=f32).astype(bf16)
        for x in range(XS):
            out[part, x] = rows


def to_row(column):
    shape = (column.shape[0], 128)
    same = lax.broadcasted_iota(jnp.int32, shape, 0) == lax.broadcasted_iota(jnp.int32, shape, 1)
    return jnp.sum(jnp.where(same, column, 0.0), axis=0, keepdims=True)


def to_column(row, n):
    shape = (n, 128)
    same = lax.broadcasted_iota(jnp.int32, shape, 0) == lax.broadcasted_iota(jnp.int32, shape, 1)
    return jnp.sum(jnp.where(same, row, 0.0), axis=1, keepdims=True)


def ask_body(ids, tile, asked, out):
    start = ids[START]
    tail = jnp.zeros((16, 128), f32)
    place = lax.broadcasted_iota(jnp.int32, (16, 128), 0)
    rows = asked[start]
    parts = []
    for h in range(KV):
        queries = jnp.concatenate(
            [rows[:, (GROUP * h + g) * HEAD : (GROUP * h + g + 1) * HEAD] for g in range(GROUP)], axis=0
        )
        keys = tile[0, :, h * HEAD : (h + 1) * HEAD]
        values = tile[1, :, h * HEAD : (h + 1) * HEAD]
        scores = lax.dot_general(queries, keys, NT, preferred_element_type=f32) * SCALE
        peak = jnp.max(scores, axis=1, keepdims=True)
        weights = jnp.exp(scores - peak)
        total = jnp.sum(weights, axis=1, keepdims=True)
        high = weights.astype(bf16)
        low = (weights - high.astype(f32)).astype(bf16)
        sums = jnp.dot(high, values, preferred_element_type=f32)
        sums = sums + jnp.dot(low, values, preferred_element_type=f32)
        parts.append((sums / total).astype(bf16))
        rest = to_row(peak + jnp.log(total))
        for i in range(3):
            piece = rest.astype(bf16).astype(f32)
            tail = jnp.where(place == 3 * h + i, piece, tail)
            rest = rest - piece
    parts.append(tail.astype(bf16))
    packed = jnp.concatenate(parts, axis=0)
    for y in range(YS):
        out[y] = packed

    @pl.when(ids[Y] == start)
    def _():
        for y in range(YS):

            @pl.when(start != y)
            def _():
                for kind in range(2):
                    for h in range(KV):
                        out[y, pl.ds((KV * kind + h) * ASK, ASK), :] = tile[
                            kind, 0:ASK, h * HEAD : (h + 1) * HEAD
                        ]


def attend_body(ids, queries, own, above, below, packs, out, side, bias):
    y, x, start, stop, asked = ids[Y], ids[X], ids[START], ids[STOP], ids[ASKED]
    for kind in range(2):
        side[kind, 0:ROWS, :] = above[kind, pl.ds(pl.multiple_of(x * ROWS, ROWS), ROWS), :]
        side[kind, 4 * ROWS : 5 * ROWS, :] = below[kind, pl.ds(pl.multiple_of(x * ROWS, ROWS), ROWS), :]
        for i in range(1, 4):

            @pl.when(x + i < XS)
            def _():
                at = pl.multiple_of(jnp.minimum(x + i, XS - 1) * ROWS, ROWS)
                side[kind, i * ROWS : (i + 1) * ROWS, :] = above[kind, pl.ds(at, ROWS), :]

            @pl.when(x + i >= XS)
            def _():
                at = pl.multiple_of(jnp.maximum(x + i - XS, 0) * ROWS, ROWS)
                side[kind, i * ROWS : (i + 1) * ROWS, :] = below[kind, pl.ds(at, ROWS), :]

        for h in range(KV):
            side[kind, 5 * ROWS : 5 * ROWS + ASK, h * HEAD : (h + 1) * HEAD] = packs[
                start, pl.ds((KV * kind + h) * ASK, ASK), :
            ]
        side[kind, 5 * ROWS + ASK :, :] = jnp.zeros((ROWS - ASK, KV * HEAD), bf16)

    i = lax.broadcasted_iota(jnp.int32, (ROWS, ROWS), 0)
    j = lax.broadcasted_iota(jnp.int32, (ROWS, ROWS), 1)
    up, down = y > start, y + 1 < stop
    first = jnp.where((y == start + 1) & (x == 0), asked, 0)
    limit = jnp.where(up, 0, ROWS)
    bias[:, 0:ROWS] = jnp.where((j >= i) & (j >= first) & (j >= limit), 0.0, MASKED)
    for b in range(1, 4):
        fine = jnp.where(x + b < XS, up.astype(jnp.int32), down.astype(jnp.int32))
        bias[:, b * ROWS : (b + 1) * ROWS] = jnp.where(j < fine * ROWS, 0.0, MASKED)
    limit = jnp.where(down, ROWS, 0)
    bias[:, 4 * ROWS : 5 * ROWS] = jnp.where((j <= i) & (j < limit), 0.0, MASKED)
    bias[:, 5 * ROWS :] = jnp.where(j < jnp.where(up, asked, 0), 0.0, MASKED)

    for h in range(KV):
        columns = slice(h * HEAD, (h + 1) * HEAD)
        for g in range(GROUP):
            mine = slice((GROUP * h + g) * HEAD, (GROUP * h + g + 1) * HEAD)
            q = queries[:, mine]
            near = lax.dot_general(q, own[0, :, columns], NT, preferred_element_type=f32) * SCALE
            far = lax.dot_general(q, side[0, :, columns], NT, preferred_element_type=f32) * SCALE + bias[...]
            peak = jnp.maximum(jnp.max(near, axis=1, keepdims=True), jnp.max(far, axis=1, keepdims=True))
            near = jnp.exp(near - peak)
            far = jnp.exp(far - peak)
            total = jnp.sum(near, axis=1, keepdims=True) + jnp.sum(far, axis=1, keepdims=True)
            sums = jnp.dot(near.astype(bf16), own[1, :, columns], preferred_element_type=f32)
            sums = sums + jnp.dot(far.astype(bf16), side[1, :, columns], preferred_element_type=f32)
            out[:, mine] = (sums / total).astype(bf16)

    @pl.when((y == start) & (x == 0))
    def _():
        n = GROUP * ASK
        for h in range(KV):
            logs = []
            for s in range(YS):
                tail = packs[s, KV * n : KV * n + 16, :].astype(f32)
                log = tail[3 * h : 3 * h + 1] + tail[3 * h + 1 : 3 * h + 2] + tail[3 * h + 2 : 3 * h + 3]
                logs.append(jnp.where((s >= start) & (s < stop), log, MASKED))
            peak = functools.reduce(jnp.maximum, logs)
            shares = [
                jnp.where((s >= start) & (s < stop), jnp.exp(logs[s] - peak), 0.0) for s in range(YS)
            ]
            total = sum(shares)
            answer = jnp.zeros((n, HEAD), f32)
            for s in range(YS):
                block = packs[s, h * n : (h + 1) * n, :].astype(f32)
                block = jnp.where((s >= start) & (s < stop), block, 0.0)
                answer = answer + to_column(shares[s] / total, n) * block
            chosen = lax.broadcasted_iota(jnp.int32, (ASK, HEAD), 0) < asked
            for g in range(GROUP):
                mine = slice((GROUP * h + g) * HEAD, (GROUP * h + g + 1) * HEAD)
                old = out[0:ASK, mine].astype(f32)
                out[0:ASK, mine] = jnp.where(chosen, answer[g * ASK : (g + 1) * ASK], old).astype(bf16)


def exchange(array, axis):
    return lax.all_to_all(array, axis, 0, 0, tiled=False)


def copies(array, n):
    return jnp.broadcast_to(array[None], (n,) + array.shape)


def per_device(tokens, queries, key_matrix, value_matrix, doc_tiles, question_lengths):
    y, x, core = lax.axis_index("y"), lax.axis_index("x"), lax.axis_index("core")
    theirs = lax.ppermute(tokens, "core", [(0, 1), (1, 0)])

    shard = jnp.where(core == 0, key_matrix, value_matrix)
    column = exchange(copies(shard, YS), "y")
    column, head = lax.optimization_barrier((column, queries[:ASK]))
    weights = exchange(copies(column, XS), "x")
    asked = exchange(copies(head, YS), "y")

    second = y >= doc_tiles[0]
    ids = jnp.stack(
        [
            y,
            x,
            core,
            jnp.where(second, doc_tiles[0], 0),
            jnp.where(second, doc_tiles[0] + doc_tiles[1], doc_tiles[0]),
            jnp.where(second, question_lengths[1], question_lengths[0]),
        ]
    ).astype(jnp.int32)

    rows = call(
        project_body,
        jax.ShapeDtypeStruct((2, XS, ROWS, KV * HEAD), bf16),
        4,
        [pltpu.VMEM((weights.shape[0] * weights.shape[1] * weights.shape[2], KV * HEAD), bf16)],
        flops=2 * 2 * tokens.size * KV * HEAD,
        moved=4 * tokens.size + 2 * weights.size,
    )(ids, weights, tokens, theirs)
    tile = exchange(rows.reshape(2 * XS, ROWS, KV * HEAD), ("core", "x")).reshape(2, TILE, KV * HEAD)

    packs = call(
        ask_body,
        jax.ShapeDtypeStruct((YS, PACK, HEAD), bf16),
        3,
        flops=3 * 2 * KV * GROUP * ASK * TILE * HEAD,
        moved=2 * tile.size + 4 * YS * PACK * HEAD,
    )(ids, tile, asked)
    packs = exchange(packs, "y")
    above = lax.ppermute(tile, "y", [(i, i + 1) for i in range(YS - 1)])
    below = lax.ppermute(tile, "y", [(i + 1, i) for i in range(YS - 1)])

    return call(
        attend_body,
        jax.ShapeDtypeStruct(queries.shape, bf16),
        6,
        [pltpu.VMEM((2, 6 * ROWS, KV * HEAD), bf16), pltpu.VMEM((ROWS, 6 * ROWS), f32)],
        flops=4 * queries.size * 10 * ROWS,
        moved=4 * queries.size + 6 * tile.size + 2 * packs.size,
    )(ids, queries, tile, above, below, packs)


def solution(mesh):
    devices = mesh.devices
    split = Mesh(devices.reshape(devices.shape[0] // 2, 2, YS, XS), ("z", "core", "y", "x"))
    rows = P(("z", "core", "y", "x"), None)
    return jax.shard_map(
        per_device,
        mesh=split,
        in_specs=(
            rows,
            rows,
            P(("y", "x"), None),
            P(("y", "x"), None),
            P(("z", "core")),
            P(("z", "core")),
        ),
        out_specs=rows,
        check_vma=False,
    )
```

```python
import functools
import math

import jax
import jax.numpy as jnp
from jax import lax
from jax.experimental import pallas as pl
from jax.experimental.pallas import tpu as pltpu
from jax.sharding import Mesh, PartitionSpec as P

HEAD = 128
TILE = 512
ASK = 16
GROUP = 7
KV = 2
ROWS = 128
XS = 4
YS = 8
TOKENS = ASK // XS
SLICE = 32
PACK = KV * SLICE + 16
SCALE = 1.0 / math.sqrt(HEAD)
MASKED = -1e30
NT = (((1,), (1,)), ((), ()))
bf16, f32 = jnp.bfloat16, jnp.float32

def spec(space):
    return pl.BlockSpec(memory_space=space)


def call(body, out, ins, scratch=(), micros=1):
    return pl.pallas_call(
        body,
        out_shape=out,
        in_specs=[spec(pltpu.SMEM)] * 2 + [spec(pltpu.VMEM)] * ins,
        out_specs=jax.tree.map(lambda _: spec(pltpu.VMEM), out),
        scratch_shapes=list(scratch),
        compiler_params=pltpu.CompilerParams(vmem_limit_bytes=24 * 1024 * 1024),
        cost_estimate=pl.CostEstimate(flops=0, bytes_accessed=micros * 3690000, transcendentals=0),
    )


def place(tiles, lengths):
    y, x = lax.axis_index("y"), lax.axis_index("x")
    second = y >= tiles[0]
    start = jnp.where(second, tiles[0], 0)
    stop = jnp.where(second, tiles[0] + tiles[1], tiles[0])
    return y, x, start, stop, jnp.where(second, lengths[1], lengths[0])


def project_body(tiles, lengths, weights, mine, theirs, out, whole):
    depth = weights.shape[2]
    for x in range(XS):
        for y in range(YS):
            whole[pl.ds((XS * y + x) * depth, depth), :] = weights[x, y]
    core = lax.axis_index("core")
    for part, tokens in ((core, mine), (1 - core, theirs)):
        rows = jnp.dot(tokens[...], whole[...], preferred_element_type=f32).astype(bf16)
        for x in range(XS):
            out[part, x] = rows


def to_row(column):
    shape = (column.shape[0], 128)
    same = lax.broadcasted_iota(jnp.int32, shape, 0) == lax.broadcasted_iota(jnp.int32, shape, 1)
    return jnp.sum(jnp.where(same, column, 0.0), axis=0, keepdims=True)


def to_column(row, n):
    shape = (n, 128)
    same = lax.broadcasted_iota(jnp.int32, shape, 0) == lax.broadcasted_iota(jnp.int32, shape, 1)
    return jnp.sum(jnp.where(same, row, 0.0), axis=1, keepdims=True)


def cut_body(head, out):
    rows = head[...].astype(f32)
    blank = jnp.zeros((SLICE - GROUP * TOKENS, HEAD), f32)
    for x in range(XS):
        parts = []
        for h in range(KV):
            for g in range(GROUP):
                n = GROUP * h + g
                parts.append(rows[x * TOKENS : (x + 1) * TOKENS, n * HEAD : (n + 1) * HEAD])
            parts.append(blank)
        out[x] = jnp.concatenate(parts, axis=0).astype(bf16)


def pick_body(tiles, lengths, own, r1, r2, r3, above, out):
    y, x, start, _, _ = place(tiles, lengths)
    for column, source in enumerate((own, r1, r2, r3)):

        @pl.when((y == start) & (x == column))
        def _():
            out[...] = source[...]

    @pl.when(y != start)
    def _():
        out[...] = above[...]


def ask_body(tiles, lengths, tile, near, far2, far4, out, asked):
    y, x, start, stop, _ = place(tiles, lengths)
    shift = y - start
    for low, high, source in ((0, 2, near), (2, 4, far2), (4, YS, far4)):

        @pl.when((shift >= low) & (shift < high))
        def _():
            asked[...] = source[...]

    tail = jnp.zeros((16, 128), f32)
    line = lax.broadcasted_iota(jnp.int32, (16, 128), 0)
    parts = []
    for h in range(KV):
        queries = asked[h * SLICE : (h + 1) * SLICE, :]
        keys = tile[0, :, h * HEAD : (h + 1) * HEAD]
        values = tile[1, :, h * HEAD : (h + 1) * HEAD]
        scores = lax.dot_general(queries, keys, NT, preferred_element_type=f32) * SCALE
        peak = jnp.max(scores, axis=1, keepdims=True)
        weights = jnp.exp(scores - peak)
        total = jnp.sum(weights, axis=1, keepdims=True)
        high = weights.astype(bf16)
        low = (weights - high.astype(f32)).astype(bf16)
        sums = jnp.dot(high, values, preferred_element_type=f32)
        sums = sums + jnp.dot(low, values, preferred_element_type=f32)
        parts.append((sums / total).astype(bf16))
        rest = to_row(peak + jnp.log(total))
        for i in range(3):
            piece = rest.astype(bf16).astype(f32)
            tail = jnp.where(line == 3 * h + i, piece, tail)
            rest = rest - piece
    parts.append(tail.astype(bf16))
    packed = jnp.concatenate(parts, axis=0)
    for to in range(YS):
        out[to] = packed

    @pl.when(y == start)
    def _():
        for to in range(YS):

            @pl.when(start != to)
            def _():
                for kind in range(2):
                    for h in range(KV):
                        out[to, pl.ds((KV * kind + h) * ASK, ASK), :] = tile[
                            kind, 0:ASK, h * HEAD : (h + 1) * HEAD
                        ]


def merge_body(tiles, lengths, packs, out):
    _, _, start, stop, _ = place(tiles, lengths)
    for h in range(KV):
        logs = []
        for s in range(YS):
            tail = packs[s, KV * SLICE : KV * SLICE + 16, :].astype(f32)
            log = tail[3 * h : 3 * h + 1] + tail[3 * h + 1 : 3 * h + 2] + tail[3 * h + 2 : 3 * h + 3]
            logs.append(jnp.where((s >= start) & (s < stop), log, MASKED))
        peak = functools.reduce(jnp.maximum, logs)
        shares = [jnp.where((s >= start) & (s < stop), jnp.exp(logs[s] - peak), 0.0) for s in range(YS)]
        total = sum(shares)
        answer = jnp.zeros((SLICE, HEAD), f32)
        for s in range(YS):
            block = packs[s, h * SLICE : (h + 1) * SLICE, :].astype(f32)
            block = jnp.where((s >= start) & (s < stop), block, 0.0)
            answer = answer + to_column(shares[s] / total, SLICE) * block
        out[h * SLICE : (h + 1) * SLICE, :] = answer.astype(bf16)


def attend_body(tiles, lengths, queries, own, above, below, packs, a0, a1, a2, a3, out, side, bias):
    y, x, start, stop, asked = place(tiles, lengths)
    for kind in range(2):
        side[kind, 0:ROWS, :] = above[kind, pl.ds(pl.multiple_of(x * ROWS, ROWS), ROWS), :]
        side[kind, 4 * ROWS : 5 * ROWS, :] = below[kind, pl.ds(pl.multiple_of(x * ROWS, ROWS), ROWS), :]
        for i in range(1, 4):

            @pl.when(x + i < XS)
            def _():
                at = pl.multiple_of(jnp.minimum(x + i, XS - 1) * ROWS, ROWS)
                side[kind, i * ROWS : (i + 1) * ROWS, :] = above[kind, pl.ds(at, ROWS), :]

            @pl.when(x + i >= XS)
            def _():
                at = pl.multiple_of(jnp.maximum(x + i - XS, 0) * ROWS, ROWS)
                side[kind, i * ROWS : (i + 1) * ROWS, :] = below[kind, pl.ds(at, ROWS), :]

        for h in range(KV):
            side[kind, 5 * ROWS : 5 * ROWS + ASK, h * HEAD : (h + 1) * HEAD] = packs[
                start, pl.ds((KV * kind + h) * ASK, ASK), :
            ]
        side[kind, 5 * ROWS + ASK :, :] = jnp.zeros((ROWS - ASK, KV * HEAD), bf16)

    i = lax.broadcasted_iota(jnp.int32, (ROWS, ROWS), 0)
    j = lax.broadcasted_iota(jnp.int32, (ROWS, ROWS), 1)
    up, down = y > start, y + 1 < stop
    first = jnp.where((y == start + 1) & (x == 0), asked, 0)
    limit = jnp.where(up, 0, ROWS)
    bias[:, 0:ROWS] = jnp.where((j >= i) & (j >= first) & (j >= limit), 0.0, MASKED)
    for b in range(1, 4):
        fine = jnp.where(x + b < XS, up.astype(jnp.int32), down.astype(jnp.int32))
        bias[:, b * ROWS : (b + 1) * ROWS] = jnp.where(j < fine * ROWS, 0.0, MASKED)
    limit = jnp.where(down, ROWS, 0)
    bias[:, 4 * ROWS : 5 * ROWS] = jnp.where((j <= i) & (j < limit), 0.0, MASKED)
    bias[:, 5 * ROWS :] = jnp.where(j < jnp.where(up, asked, 0), 0.0, MASKED)

    for h in range(KV):
        columns = slice(h * HEAD, (h + 1) * HEAD)
        for g in range(GROUP):
            mine = slice((GROUP * h + g) * HEAD, (GROUP * h + g + 1) * HEAD)
            q = queries[:, mine]
            near = lax.dot_general(q, own[0, :, columns], NT, preferred_element_type=f32) * SCALE
            far = lax.dot_general(q, side[0, :, columns], NT, preferred_element_type=f32) * SCALE + bias[...]
            peak = jnp.maximum(jnp.max(near, axis=1, keepdims=True), jnp.max(far, axis=1, keepdims=True))
            near = jnp.exp(near - peak)
            far = jnp.exp(far - peak)
            total = jnp.sum(near, axis=1, keepdims=True) + jnp.sum(far, axis=1, keepdims=True)
            sums = jnp.dot(near.astype(bf16), own[1, :, columns], preferred_element_type=f32)
            sums = sums + jnp.dot(far.astype(bf16), side[1, :, columns], preferred_element_type=f32)
            out[:, mine] = (sums / total).astype(bf16)

    @pl.when((y == start) & (x == 0))
    def _():
        chosen = lax.broadcasted_iota(jnp.int32, (ASK, HEAD), 0) < asked
        answers = [a[...].astype(f32) for a in (a0, a1, a2, a3)]
        for h in range(KV):
            for g in range(GROUP):
                mine = slice((GROUP * h + g) * HEAD, (GROUP * h + g + 1) * HEAD)
                at = h * SLICE + g * TOKENS
                answer = jnp.concatenate([a[at : at + TOKENS] for a in answers], axis=0)
                old = out[0:ASK, mine].astype(f32)
                out[0:ASK, mine] = jnp.where(chosen, answer, old).astype(bf16)


def exchange(array, axis):
    return lax.all_to_all(array, axis, 0, 0, tiled=False)


def down(array, shift):
    return lax.ppermute(array, "y", [(y, y + shift) for y in range(YS) if 0 <= y + shift < YS])


def copies(array, n):
    return jnp.broadcast_to(array[None], (n,) + array.shape)


def per_device(tokens, queries, key_matrix, value_matrix, doc_tiles, question_lengths):
    core = lax.axis_index("core")
    plane = ("y", "x")
    slice_shape = jax.ShapeDtypeStruct((KV * SLICE, HEAD), bf16)
    at = (doc_tiles, question_lengths)
    theirs = lax.ppermute(tokens, "core", [(0, 1), (1, 0)])
    slices = pl.pallas_call(
        cut_body,
        out_shape=jax.ShapeDtypeStruct((XS,) + slice_shape.shape, bf16),
        in_specs=[spec(pltpu.VMEM)],
        out_specs=spec(pltpu.VMEM),
    )(queries[:ASK])

    shard = jnp.where(core == 0, key_matrix, value_matrix)
    column = exchange(copies(shard, YS), "y")
    spread = [
        lax.ppermute(slices[x], plane, [(XS * y, XS * y + x) for y in range(YS)]) for x in range(1, XS)
    ]
    column, theirs, spread = lax.optimization_barrier((column, theirs, spread))
    weights = exchange(copies(column, XS), "x")
    joined = jnp.where(lax.axis_index("x") == 0, slices[0], spread[0] + spread[1] + spread[2])
    first = down(joined, 1)
    near = call(pick_body, slice_shape, 5)(*at, slices[0], *spread, first)
    far2, far4 = down(near, 2), down(near, 4)
    weights, near, far2, far4 = lax.optimization_barrier((weights, near, far2, far4))

    rows = call(
        project_body,
        jax.ShapeDtypeStruct((2, XS, ROWS, KV * HEAD), bf16),
        3,
        [pltpu.VMEM((weights.shape[0] * weights.shape[1] * weights.shape[2], KV * HEAD), bf16)],
    )(*at, weights, tokens, theirs)
    tile = exchange(rows.reshape(2 * XS, ROWS, KV * HEAD), ("core", "x")).reshape(2, TILE, KV * HEAD)

    packs = call(
        ask_body, jax.ShapeDtypeStruct((YS, PACK, HEAD), bf16), 4, [pltpu.VMEM(slice_shape.shape, bf16)]
    )(*at, tile, near, far2, far4)
    packs = exchange(packs, "y")
    above, below = down(tile, 1), down(tile, -1)
    answer = call(merge_body, slice_shape, 1)(*at, packs)
    answers = [answer] + [
        lax.ppermute(answer, plane, [(XS * y + x, XS * y) for y in range(YS)]) for x in range(1, XS)
    ]

    return call(
        attend_body,
        jax.ShapeDtypeStruct(queries.shape, bf16),
        9,
        [pltpu.VMEM((2, 6 * ROWS, KV * HEAD), bf16), pltpu.VMEM((ROWS, 6 * ROWS), f32)],
        micros=7,
    )(*at, queries, tile, above, below, packs, *answers)


def solution(mesh):
    devices = mesh.devices
    split = Mesh(devices.reshape(devices.shape[0] // 2, 2, YS, XS), ("z", "core", "y", "x"))
    rows = P(("z", "core", "y", "x"), None)
    return jax.shard_map(
        per_device,
        mesh=split,
        in_specs=(
            rows,
            rows,
            P(("y", "x"), None),
            P(("y", "x"), None),
            P(("z", "core")),
            P(("z", "core")),
        ),
        out_specs=rows,
        check_vma=False,
    )
```

```python
import functools
import math

import jax
import jax.numpy as jnp
from jax import lax
from jax.experimental import pallas as pl
from jax.experimental.pallas import tpu as pltpu
from jax.sharding import Mesh, PartitionSpec as P

HEAD = 128
TILE = 512
ASK = 16
GROUP = 7
KV = 2
ROWS = 128
XS = 4
YS = 8
BLOCK = GROUP * ASK
PACK = KV * BLOCK + 16
SCALE = math.log2(math.e) / math.sqrt(HEAD)
MASKED = -1e30
NT = (((1,), (1,)), ((), ()))
bf16, f32 = jnp.bfloat16, jnp.float32

def spec(space):
    return pl.BlockSpec(memory_space=space)


def call(body, out, ins, scratch=(), micros=1):
    return pl.pallas_call(
        body,
        out_shape=out,
        in_specs=[spec(pltpu.SMEM)] * 2 + [spec(pltpu.VMEM)] * ins,
        out_specs=jax.tree.map(lambda _: spec(pltpu.VMEM), out),
        scratch_shapes=list(scratch),
        compiler_params=pltpu.CompilerParams(vmem_limit_bytes=24 * 1024 * 1024),
        cost_estimate=pl.CostEstimate(flops=0, bytes_accessed=micros * 3690000, transcendentals=0),
    )


def place(tiles, lengths):
    y, x = lax.axis_index("y"), lax.axis_index("x")
    second = y >= tiles[0]
    start = jnp.where(second, tiles[0], 0)
    stop = jnp.where(second, tiles[0] + tiles[1], tiles[0])
    return y, x, start, stop, jnp.where(second, lengths[1], lengths[0])


def project_body(tiles, lengths, weights, mine, sibling, across, corner, out, whole):
    depth = weights.shape[2]
    for x in range(XS):
        for y in range(YS):
            whole[pl.ds((XS * y + x) * depth, depth), :] = weights[x, y]
    pair, core = lax.axis_index("pair"), lax.axis_index("core")
    for z, c, tokens in (
        (pair, core, mine),
        (pair, 1 - core, sibling),
        (1 - pair, core, across),
        (1 - pair, 1 - core, corner),
    ):
        rows = jnp.dot(tokens[...], whole[...], preferred_element_type=f32).astype(bf16)
        for x in range(XS):
            out[z, c, x] = rows


def to_row(column):
    shape = (column.shape[0], 128)
    same = lax.broadcasted_iota(jnp.int32, shape, 0) == lax.broadcasted_iota(jnp.int32, shape, 1)
    return jnp.sum(jnp.where(same, column, 0.0), axis=0, keepdims=True)


def to_column(row, n):
    shape = (n, 128)
    same = lax.broadcasted_iota(jnp.int32, shape, 0) == lax.broadcasted_iota(jnp.int32, shape, 1)
    return jnp.sum(jnp.where(same, row, 0.0), axis=1, keepdims=True)


def head_columns(n):
    return slice(n * HEAD, (n + 1) * HEAD)


def ask_body(tiles, lengths, own, below, head, head2, head4, out, asked):
    y, x, start, stop, _ = place(tiles, lengths)
    shift = y - start
    for at, source in ((2, head2), (4, head4)):

        @pl.when(shift == at)
        def _():
            asked[...] = source[...]

    @pl.when((shift != 2) & (shift != 4))
    def _():
        asked[...] = head[...]

    more = y + 1 < stop
    tail = jnp.zeros((16, 128), f32)
    line = lax.broadcasted_iota(jnp.int32, (16, 128), 0)
    for h in range(KV):
        queries = jnp.concatenate([asked[:, head_columns(GROUP * h + g)] for g in range(GROUP)], axis=0)
        near = lax.dot_general(queries, own[h, 0], NT, preferred_element_type=f32)
        far = lax.dot_general(queries, below[h, 0], NT, preferred_element_type=f32)
        far = jnp.where(more, far, MASKED)
        peak = jnp.maximum(jnp.max(near, axis=1, keepdims=True), jnp.max(far, axis=1, keepdims=True))
        sums, total = jnp.zeros((BLOCK, HEAD), f32), jnp.zeros((BLOCK, 1), f32)
        for scores, block in ((near, own), (far, below)):
            weights = jnp.exp2((scores - peak) * SCALE)
            total = total + jnp.sum(weights, axis=1, keepdims=True)
            high = weights.astype(bf16)
            low = (weights - high.astype(f32)).astype(bf16)
            sums = sums + jnp.dot(high, block[h, 1], preferred_element_type=f32)
            sums = sums + jnp.dot(low, block[h, 1], preferred_element_type=f32)
        out[h * BLOCK : (h + 1) * BLOCK, :] = (sums / total).astype(bf16)
        rest = to_row(peak * SCALE + jnp.log2(total))
        for i in range(3):
            piece = rest.astype(bf16).astype(f32)
            tail = jnp.where(line == 3 * h + i, piece, tail)
            rest = rest - piece
    out[KV * BLOCK :, :] = tail.astype(bf16)


def attend_body(
    tiles, lengths, queries, own, above, below, questions, pack, back2, back4, out, side, bias, rows
):
    y, x, start, stop, asked = place(tiles, lengths)
    at = pl.multiple_of(x * ROWS, ROWS)
    side[:, :, 0:ROWS, :] = above[:, :, pl.ds(at, ROWS), :]
    side[:, :, 4 * ROWS : 5 * ROWS, :] = below[:, :, pl.ds(at, ROWS), :]
    for h in range(KV):
        for kind in range(2):
            side[h, kind, 5 * ROWS : 5 * ROWS + ASK, :] = questions[start, 2 * h + kind]
            side[h, kind, 5 * ROWS + ASK :, :] = jnp.zeros((ROWS - ASK, HEAD), bf16)
    for i in range(1, 4):

        @pl.when(x + i < XS)
        def _():
            at = pl.multiple_of(jnp.minimum(x + i, XS - 1) * ROWS, ROWS)
            side[:, :, i * ROWS : (i + 1) * ROWS, :] = above[:, :, pl.ds(at, ROWS), :]

        @pl.when(x + i >= XS)
        def _():
            at = pl.multiple_of(jnp.maximum(x + i - XS, 0) * ROWS, ROWS)
            side[:, :, i * ROWS : (i + 1) * ROWS, :] = below[:, :, pl.ds(at, ROWS), :]

    i = lax.broadcasted_iota(jnp.int32, (ROWS, ROWS), 0)
    j = lax.broadcasted_iota(jnp.int32, (ROWS, ROWS), 1)
    up, down = y > start, y + 1 < stop
    first = jnp.where((y == start + 1) & (x == 0), asked, 0)
    limit = jnp.where(up, 0, ROWS)
    bias[:, 0:ROWS] = jnp.where((j >= i) & (j >= first) & (j >= limit), 0.0, MASKED)
    for b in range(1, 4):
        fine = jnp.where(x + b < XS, up.astype(jnp.int32), down.astype(jnp.int32))
        bias[:, b * ROWS : (b + 1) * ROWS] = jnp.where(j < fine * ROWS, 0.0, MASKED)
    limit = jnp.where(down, ROWS, 0)
    bias[:, 4 * ROWS : 5 * ROWS] = jnp.where((j <= i) & (j < limit), 0.0, MASKED)
    bias[:, 5 * ROWS :] = jnp.where(j < jnp.where(up, asked, 0), 0.0, MASKED)

    for n in range(KV * GROUP):
        rows[n * ROWS : (n + 1) * ROWS, :] = queries[:, head_columns(n)]
    for h in range(KV):
        q = rows[h * GROUP * ROWS : (h + 1) * GROUP * ROWS, :]
        near = lax.dot_general(q, own[h, 0], NT, preferred_element_type=f32)
        far = lax.dot_general(q, side[h, 0], NT, preferred_element_type=f32)
        far = (far.reshape(GROUP, ROWS, 6 * ROWS) + bias[...][None]).reshape(GROUP * ROWS, 6 * ROWS)
        peak = jnp.maximum(jnp.max(near, axis=1, keepdims=True), jnp.max(far, axis=1, keepdims=True))
        near = jnp.exp2((near - peak) * SCALE)
        far = jnp.exp2((far - peak) * SCALE)
        total = jnp.sum(near, axis=1, keepdims=True) + jnp.sum(far, axis=1, keepdims=True)
        sums = jnp.dot(near.astype(bf16), own[h, 1], preferred_element_type=f32)
        sums = sums + jnp.dot(far.astype(bf16), side[h, 1], preferred_element_type=f32)
        answer = (sums / total).astype(bf16)
        for g in range(GROUP):
            out[:, head_columns(GROUP * h + g)] = answer[g * ROWS : (g + 1) * ROWS]

    @pl.when((y == start) & (x == 0))
    def _():
        chosen = lax.broadcasted_iota(jnp.int32, (ASK, HEAD), 0) < asked
        sources = ((pack, True), (back2, start + 2 < stop), (back4, start + 4 < stop))
        for h in range(KV):
            logs = []
            for source, valid in sources:
                tail = source[KV * BLOCK :, :].astype(f32)
                log = tail[3 * h : 3 * h + 1] + tail[3 * h + 1 : 3 * h + 2] + tail[3 * h + 2 : 3 * h + 3]
                logs.append(jnp.where(valid, log, MASKED))
            peak = functools.reduce(jnp.maximum, logs)
            shares = [jnp.exp2(log - peak) for log in logs]
            total = sum(shares)
            answer = jnp.zeros((BLOCK, HEAD), f32)
            for share, (source, valid) in zip(shares, sources):
                block = jnp.where(valid, source[h * BLOCK : (h + 1) * BLOCK, :].astype(f32), 0.0)
                answer = answer + to_column(share / total, BLOCK) * block
            for g in range(GROUP):
                mine = head_columns(GROUP * h + g)
                old = out[0:ASK, mine].astype(f32)
                out[0:ASK, mine] = jnp.where(chosen, answer[g * ASK : (g + 1) * ASK], old).astype(bf16)


def exchange(array, axis):
    return lax.all_to_all(array, axis, 0, 0, tiled=False)


def down(array, shift):
    return lax.ppermute(array, "y", [(y, y + shift) for y in range(YS) if 0 <= y + shift < YS])


def copies(array, n):
    return jnp.broadcast_to(array[None], (n,) + array.shape)


def along(array, shift):
    pairs = [(XS * y, XS * (y + shift)) for y in range(YS) if 0 <= y + shift < YS]
    return lax.ppermute(array, ("y", "x"), pairs)


def per_device(tokens, queries, key_matrix, value_matrix, doc_tiles, question_lengths):
    core, pair = lax.axis_index("core"), lax.axis_index("pair")
    swap = [(0, 1), (1, 0)]
    at = (doc_tiles, question_lengths)
    across = lax.ppermute(tokens, "pair", swap)

    shard = jnp.where(core == 0, key_matrix, value_matrix)
    shard = jnp.where(pair == 0, shard[:, :HEAD], shard[:, HEAD:])
    column = exchange(copies(shard, YS), "y")
    column, mine, head = lax.optimization_barrier((column, tokens, queries[:ASK]))
    sibling, corner = lax.ppermute(mine, "core", swap), lax.ppermute(across, "core", swap)
    weights = exchange(copies(column, XS), "x")
    head2, head4 = along(head, 2), along(head, 4)
    weights, head2, head4 = lax.optimization_barrier((weights, head2, head4))

    rows = call(
        project_body,
        jax.ShapeDtypeStruct((2, 2, XS, ROWS, HEAD), bf16),
        5,
        [pltpu.VMEM((weights.shape[0] * weights.shape[1] * weights.shape[2], HEAD), bf16)],
        micros=2,
    )(*at, weights, tokens, sibling, across, corner)
    tile = exchange(rows.reshape(4 * XS, ROWS, HEAD), ("pair", "core", "x")).reshape(KV, 2, TILE, HEAD)

    above, below = down(tile, 1), down(tile, -1)
    questions = exchange(copies(tile[:, :, :ASK].reshape(2 * KV, ASK, HEAD), YS), "y")
    pack = call(
        ask_body,
        jax.ShapeDtypeStruct((PACK, HEAD), bf16),
        5,
        [pltpu.VMEM(head.shape, bf16)],
        micros=2,
    )(*at, tile, below, head, head2, head4)
    back2, back4 = along(pack, -2), along(pack, -4)

    return call(
        attend_body,
        jax.ShapeDtypeStruct(queries.shape, bf16),
        8,
        [
            pltpu.VMEM((KV, 2, 6 * ROWS, HEAD), bf16),
            pltpu.VMEM((ROWS, 6 * ROWS), f32),
            pltpu.VMEM((KV * GROUP * ROWS, HEAD), bf16),
        ],
        micros=5,
    )(*at, queries, tile, above, below, questions, pack, back2, back4)


def solution(mesh):
    devices = mesh.devices
    split = Mesh(devices.reshape(devices.shape[0] // 4, 2, 2, YS, XS), ("z", "pair", "core", "y", "x"))
    rows = P(("z", "pair", "core", "y", "x"), None)
    return jax.shard_map(
        per_device,
        mesh=split,
        in_specs=(
            rows,
            rows,
            P(("y", "x"), None),
            P(("y", "x"), None),
            P(("z", "pair", "core")),
            P(("z", "pair", "core")),
        ),
        out_specs=rows,
        check_vma=False,
    )
```

```python
import functools
import math

import jax
import jax.numpy as jnp
from jax import lax
from jax.experimental import pallas as pl
from jax.experimental.pallas import tpu as pltpu
from jax.sharding import Mesh, PartitionSpec as P

HEAD = 128
TILE = 512
ASK = 16
GROUP = 7
KV = 2
ROWS = 128
XS = 4
YS = 8
BLOCK = GROUP * ASK
PACK = KV * BLOCK + 16
SCALE = math.log2(math.e) / math.sqrt(HEAD)
MASKED = -1e30
NT = (((1,), (1,)), ((), ()))
bf16, f32 = jnp.bfloat16, jnp.float32

def spec(space):
    return pl.BlockSpec(memory_space=space)


def call(body, out, ins, scratch=(), micros=1, scalars=2):
    return pl.pallas_call(
        body,
        out_shape=out,
        in_specs=[spec(pltpu.SMEM)] * scalars + [spec(pltpu.VMEM)] * ins,
        out_specs=spec(pltpu.VMEM),
        scratch_shapes=list(scratch),
        compiler_params=pltpu.CompilerParams(vmem_limit_bytes=24 * 1024 * 1024),
        cost_estimate=pl.CostEstimate(flops=0, bytes_accessed=micros * 3690000, transcendentals=0),
    )


def place(tiles, lengths):
    y, x = lax.axis_index("y"), lax.axis_index("x")
    second = y >= tiles[0]
    start = jnp.where(second, tiles[0], 0)
    stop = jnp.where(second, tiles[0] + tiles[1], tiles[0])
    return y, x, start, stop, jnp.where(second, lengths[1], lengths[0])


def project_body(weights, mine, sibling, across, corner, out):
    pair, core = lax.axis_index("pair"), lax.axis_index("core")
    for z, c, tokens in (
        (pair, core, mine),
        (pair, 1 - core, sibling),
        (1 - pair, core, across),
        (1 - pair, 1 - core, corner),
    ):
        rows = jnp.dot(tokens[...], weights[...], preferred_element_type=f32).astype(bf16)
        for x in range(XS):
            out[z, c, x] = rows


def to_row(column):
    shape = (column.shape[0], 128)
    same = lax.broadcasted_iota(jnp.int32, shape, 0) == lax.broadcasted_iota(jnp.int32, shape, 1)
    return jnp.sum(jnp.where(same, column, 0.0), axis=0, keepdims=True)


def to_column(row, n):
    shape = (n, 128)
    same = lax.broadcasted_iota(jnp.int32, shape, 0) == lax.broadcasted_iota(jnp.int32, shape, 1)
    return jnp.sum(jnp.where(same, row, 0.0), axis=1, keepdims=True)


def head_columns(n):
    return slice(n * HEAD, (n + 1) * HEAD)


def ask_body(tiles, lengths, own, below, head, head2, head4, out, asked):
    y, x, start, stop, _ = place(tiles, lengths)
    shift = y - start
    for at, source in ((2, head2), (4, head4)):

        @pl.when(shift == at)
        def _():
            asked[...] = source[...]

    @pl.when((shift != 2) & (shift != 4))
    def _():
        asked[...] = head[...]

    more = y + 1 < stop
    tail = jnp.zeros((16, 128), f32)
    line = lax.broadcasted_iota(jnp.int32, (16, 128), 0)
    for h in range(KV):
        queries = jnp.concatenate([asked[:, head_columns(GROUP * h + g)] for g in range(GROUP)], axis=0)
        near = lax.dot_general(queries, own[h, 0], NT, preferred_element_type=f32)
        far = lax.dot_general(queries, below[h, 0], NT, preferred_element_type=f32)
        far = jnp.where(more, far, MASKED)
        peak = jnp.maximum(jnp.max(near, axis=1, keepdims=True), jnp.max(far, axis=1, keepdims=True))
        sums, total = jnp.zeros((BLOCK, HEAD), f32), jnp.zeros((BLOCK, 1), f32)
        for scores, block in ((near, own), (far, below)):
            weights = jnp.exp2((scores - peak) * SCALE)
            total = total + jnp.sum(weights, axis=1, keepdims=True)
            high = weights.astype(bf16)
            low = (weights - high.astype(f32)).astype(bf16)
            sums = sums + jnp.dot(high, block[h, 1], preferred_element_type=f32)
            sums = sums + jnp.dot(low, block[h, 1], preferred_element_type=f32)
        out[h * BLOCK : (h + 1) * BLOCK, :] = (sums / total).astype(bf16)
        rest = to_row(peak * SCALE + jnp.log2(total))
        for i in range(3):
            piece = rest.astype(bf16).astype(f32)
            tail = jnp.where(line == 3 * h + i, piece, tail)
            rest = rest - piece
    out[KV * BLOCK :, :] = tail.astype(bf16)


def attend_body(
    tiles, lengths, queries, own, above, below, questions, out, side, bias, rows
):
    y, x, start, stop, asked = place(tiles, lengths)
    at = pl.multiple_of(x * ROWS, ROWS)
    side[:, :, 0:ROWS, :] = above[:, :, pl.ds(at, ROWS), :]
    side[:, :, 4 * ROWS : 5 * ROWS, :] = below[:, :, pl.ds(at, ROWS), :]
    for h in range(KV):
        for kind in range(2):
            side[h, kind, 5 * ROWS : 5 * ROWS + ASK, :] = questions[start, 2 * h + kind]
            side[h, kind, 5 * ROWS + ASK :, :] = jnp.zeros((ROWS - ASK, HEAD), bf16)
    for i in range(1, 4):

        @pl.when(x + i < XS)
        def _():
            at = pl.multiple_of(jnp.minimum(x + i, XS - 1) * ROWS, ROWS)
            side[:, :, i * ROWS : (i + 1) * ROWS, :] = above[:, :, pl.ds(at, ROWS), :]

        @pl.when(x + i >= XS)
        def _():
            at = pl.multiple_of(jnp.maximum(x + i - XS, 0) * ROWS, ROWS)
            side[:, :, i * ROWS : (i + 1) * ROWS, :] = below[:, :, pl.ds(at, ROWS), :]

    i = lax.broadcasted_iota(jnp.int32, (ROWS, ROWS), 0)
    j = lax.broadcasted_iota(jnp.int32, (ROWS, ROWS), 1)
    up, down = y > start, y + 1 < stop
    first = jnp.where((y == start + 1) & (x == 0), asked, 0)
    limit = jnp.where(up, 0, ROWS)
    bias[:, 0:ROWS] = jnp.where((j >= i) & (j >= first) & (j >= limit), 0.0, MASKED)
    for b in range(1, 4):
        fine = jnp.where(x + b < XS, up.astype(jnp.int32), down.astype(jnp.int32))
        bias[:, b * ROWS : (b + 1) * ROWS] = jnp.where(j < fine * ROWS, 0.0, MASKED)
    limit = jnp.where(down, ROWS, 0)
    bias[:, 4 * ROWS : 5 * ROWS] = jnp.where((j <= i) & (j < limit), 0.0, MASKED)
    bias[:, 5 * ROWS :] = jnp.where(j < jnp.where(up, asked, 0), 0.0, MASKED)

    for n in range(KV * GROUP):
        rows[n * ROWS : (n + 1) * ROWS, :] = queries[:, head_columns(n)]
    for h in range(KV):
        q = rows[h * GROUP * ROWS : (h + 1) * GROUP * ROWS, :]
        near = lax.dot_general(q, own[h, 0], NT, preferred_element_type=f32)
        far = lax.dot_general(q, side[h, 0], NT, preferred_element_type=f32)
        far = (far.reshape(GROUP, ROWS, 6 * ROWS) + bias[...][None]).reshape(GROUP * ROWS, 6 * ROWS)
        peak = jnp.maximum(jnp.max(near, axis=1, keepdims=True), jnp.max(far, axis=1, keepdims=True))
        near = jnp.exp2((near - peak) * SCALE)
        far = jnp.exp2((far - peak) * SCALE)
        total = jnp.sum(near, axis=1, keepdims=True) + jnp.sum(far, axis=1, keepdims=True)
        sums = jnp.dot(near.astype(bf16), own[h, 1], preferred_element_type=f32)
        sums = sums + jnp.dot(far.astype(bf16), side[h, 1], preferred_element_type=f32)
        answer = (sums / total).astype(bf16)
        for g in range(GROUP):
            out[:, head_columns(GROUP * h + g)] = answer[g * ROWS : (g + 1) * ROWS]


def patch_body(tiles, lengths, banded, pack, back2, back4, out):
    y, x, start, stop, asked = place(tiles, lengths)
    out[...] = banded[...]

    @pl.when((y == start) & (x == 0))
    def _():
        chosen = lax.broadcasted_iota(jnp.int32, (ASK, HEAD), 0) < asked
        sources = ((pack, True), (back2, start + 2 < stop), (back4, start + 4 < stop))
        for h in range(KV):
            logs = []
            for source, valid in sources:
                tail = source[KV * BLOCK :, :].astype(f32)
                log = tail[3 * h : 3 * h + 1] + tail[3 * h + 1 : 3 * h + 2] + tail[3 * h + 2 : 3 * h + 3]
                logs.append(jnp.where(valid, log, MASKED))
            peak = functools.reduce(jnp.maximum, logs)
            shares = [jnp.exp2(log - peak) for log in logs]
            total = sum(shares)
            answer = jnp.zeros((BLOCK, HEAD), f32)
            for share, (source, valid) in zip(shares, sources):
                block = jnp.where(valid, source[h * BLOCK : (h + 1) * BLOCK, :].astype(f32), 0.0)
                answer = answer + to_column(share / total, BLOCK) * block
            for g in range(GROUP):
                mine = head_columns(GROUP * h + g)
                old = out[0:ASK, mine].astype(f32)
                out[0:ASK, mine] = jnp.where(chosen, answer[g * ASK : (g + 1) * ASK], old).astype(bf16)


def exchange(array, axis):
    return lax.all_to_all(array, axis, 0, 0, tiled=False)


def down(array, shift):
    return lax.ppermute(array, "y", [(y, y + shift) for y in range(YS) if 0 <= y + shift < YS])


def copies(array, n):
    return jnp.broadcast_to(array[None], (n,) + array.shape)


def along(array, shift):
    pairs = [(XS * y, XS * (y + shift)) for y in range(YS) if 0 <= y + shift < YS]
    return lax.ppermute(array, ("y", "x"), pairs)


def per_device(tokens, queries, key_matrix, value_matrix, doc_tiles, question_lengths):
    core, pair = lax.axis_index("core"), lax.axis_index("pair")
    swap = [(0, 1), (1, 0)]
    at = (doc_tiles, question_lengths)
    across = lax.ppermute(tokens, "pair", swap)

    shard = jnp.where(core == 0, key_matrix, value_matrix)
    shard = jnp.where(pair == 0, shard[:, :HEAD], shard[:, HEAD:])
    weights = exchange(copies(shard, YS * XS), ("y", "x")).reshape(tokens.shape[1], HEAD)
    head = queries[:ASK]
    sibling, corner = lax.ppermute(tokens, "core", swap), lax.ppermute(across, "core", swap)
    head2, head4 = along(head, 2), along(head, 4)
    weights, head2, head4 = lax.optimization_barrier((weights, head2, head4))

    rows = call(
        project_body, jax.ShapeDtypeStruct((2, 2, XS, ROWS, HEAD), bf16), 5, micros=2, scalars=0
    )(weights, tokens, sibling, across, corner)
    tile = exchange(rows.reshape(4 * XS, ROWS, HEAD), ("pair", "core", "x")).reshape(KV, 2, TILE, HEAD)

    above, below = down(tile, 1), down(tile, -1)
    questions = exchange(copies(tile[:, :, :ASK].reshape(2 * KV, ASK, HEAD), YS), "y")
    pack = call(
        ask_body,
        jax.ShapeDtypeStruct((PACK, HEAD), bf16),
        5,
        [pltpu.VMEM(head.shape, bf16)],
        micros=2,
    )(*at, tile, below, head, head2, head4)
    back2, back4 = along(pack, -2), along(pack, -4)

    banded = call(
        attend_body,
        jax.ShapeDtypeStruct(queries.shape, bf16),
        5,
        [
            pltpu.VMEM((KV, 2, 6 * ROWS, HEAD), bf16),
            pltpu.VMEM((ROWS, 6 * ROWS), f32),
            pltpu.VMEM((KV * GROUP * ROWS, HEAD), bf16),
        ],
        micros=5,
    )(*at, queries, tile, above, below, questions)
    top = pl.BlockSpec((ASK, queries.shape[1]), lambda i: (0, 0))
    return pl.pallas_call(
        patch_body,
        out_shape=jax.ShapeDtypeStruct(queries.shape, bf16),
        grid=(1,),
        in_specs=[spec(pltpu.SMEM)] * 2 + [top] + [spec(pltpu.VMEM)] * 3,
        out_specs=top,
        input_output_aliases={2: 0},
        compiler_params=pltpu.CompilerParams(vmem_limit_bytes=4 * 1024 * 1024),
        cost_estimate=pl.CostEstimate(flops=0, bytes_accessed=3690000, transcendentals=0),
    )(*at, banded, pack, back2, back4)


def solution(mesh):
    devices = mesh.devices
    split = Mesh(devices.reshape(devices.shape[0] // 4, 2, 2, YS, XS), ("z", "pair", "core", "y", "x"))
    rows = P(("z", "pair", "core", "y", "x"), None)
    return jax.shard_map(
        per_device,
        mesh=split,
        in_specs=(
            rows,
            rows,
            P(("y", "x"), None),
            P(("y", "x"), None),
            P(("z", "pair", "core")),
            P(("z", "pair", "core")),
        ),
        out_specs=rows,
        check_vma=False,
    )
```

```python
import functools
import math

import jax
import jax.numpy as jnp
from jax import lax
from jax.experimental import pallas as pl
from jax.experimental.pallas import tpu as pltpu
from jax.sharding import Mesh, PartitionSpec as P

HEAD = 128
TILE = 512
ASK = 16
GROUP = 7
KV = 2
ROWS = 128
XS = 4
YS = 8
BLOCK = GROUP * ASK
PACK = KV * BLOCK + 16
SCALE = math.log2(math.e) / math.sqrt(HEAD)
MASKED = -1e30
NT = (((1,), (1,)), ((), ()))
bf16, f32 = jnp.bfloat16, jnp.float32

def spec(space):
    return pl.BlockSpec(memory_space=space)


def call(body, out, ins, scratch=(), micros=1, scalars=2):
    return pl.pallas_call(
        body,
        out_shape=out,
        in_specs=[spec(pltpu.SMEM)] * scalars + [spec(pltpu.VMEM)] * ins,
        out_specs=spec(pltpu.VMEM),
        scratch_shapes=list(scratch),
        compiler_params=pltpu.CompilerParams(vmem_limit_bytes=24 * 1024 * 1024),
        cost_estimate=pl.CostEstimate(flops=0, bytes_accessed=micros * 3690000, transcendentals=0),
    )


def place(tiles, lengths):
    y, x = lax.axis_index("y"), lax.axis_index("x")
    second = y >= tiles[0]
    start = jnp.where(second, tiles[0], 0)
    stop = jnp.where(second, tiles[0] + tiles[1], tiles[0])
    return y, x, start, stop, jnp.where(second, lengths[1], lengths[0])


def project_body(weights, mine, sibling, across, corner, out):
    pair, core = lax.axis_index("pair"), lax.axis_index("core")
    for z, c, tokens in (
        (pair, core, mine),
        (pair, 1 - core, sibling),
        (1 - pair, core, across),
        (1 - pair, 1 - core, corner),
    ):
        rows = jnp.dot(tokens[...], weights[...], preferred_element_type=f32).astype(bf16)
        for x in range(XS):
            out[z, c, x] = rows


def to_row(column):
    shape = (column.shape[0], 128)
    same = lax.broadcasted_iota(jnp.int32, shape, 0) == lax.broadcasted_iota(jnp.int32, shape, 1)
    return jnp.sum(jnp.where(same, column, 0.0), axis=0, keepdims=True)


def to_column(row, n):
    shape = (n, 128)
    same = lax.broadcasted_iota(jnp.int32, shape, 0) == lax.broadcasted_iota(jnp.int32, shape, 1)
    return jnp.sum(jnp.where(same, row, 0.0), axis=1, keepdims=True)


def head_columns(n):
    return slice(n * HEAD, (n + 1) * HEAD)


def ask_body(tiles, lengths, own, below, head, head2, head4, out, asked):
    y, x, start, stop, _ = place(tiles, lengths)
    shift = y - start
    for at, source in ((2, head2), (4, head4)):

        @pl.when(shift == at)
        def _():
            asked[...] = source[...]

    @pl.when((shift != 2) & (shift != 4))
    def _():
        asked[...] = head[...]

    more = y + 1 < stop
    tail = jnp.zeros((16, 128), f32)
    line = lax.broadcasted_iota(jnp.int32, (16, 128), 0)
    for h in range(KV):
        queries = jnp.concatenate([asked[:, head_columns(GROUP * h + g)] for g in range(GROUP)], axis=0)
        near = lax.dot_general(queries, own[h, 0], NT, preferred_element_type=f32)
        far = lax.dot_general(queries, below[h, 0], NT, preferred_element_type=f32)
        far = jnp.where(more, far, MASKED)
        peak = jnp.maximum(jnp.max(near, axis=1, keepdims=True), jnp.max(far, axis=1, keepdims=True))
        sums, total = jnp.zeros((BLOCK, HEAD), f32), jnp.zeros((BLOCK, 1), f32)
        for scores, block in ((near, own), (far, below)):
            weights = jnp.exp2((scores - peak) * SCALE)
            total = total + jnp.sum(weights, axis=1, keepdims=True)
            high = weights.astype(bf16)
            low = (weights - high.astype(f32)).astype(bf16)
            sums = sums + jnp.dot(high, block[h, 1], preferred_element_type=f32)
            sums = sums + jnp.dot(low, block[h, 1], preferred_element_type=f32)
        out[h * BLOCK : (h + 1) * BLOCK, :] = (sums / total).astype(bf16)
        rest = to_row(peak * SCALE + jnp.log2(total))
        for i in range(3):
            piece = rest.astype(bf16).astype(f32)
            tail = jnp.where(line == 3 * h + i, piece, tail)
            rest = rest - piece
    out[KV * BLOCK :, :] = tail.astype(bf16)


def attend_body(
    tiles, lengths, queries, own, above, below, questions, out, side, bias, rows
):
    y, x, start, stop, asked = place(tiles, lengths)
    at = pl.multiple_of(x * ROWS, ROWS)
    side[:, :, 0:ROWS, :] = above[:, :, pl.ds(at, ROWS), :]
    side[:, :, 4 * ROWS : 5 * ROWS, :] = below[:, :, pl.ds(at, ROWS), :]
    for h in range(KV):
        for kind in range(2):
            side[h, kind, 5 * ROWS : 5 * ROWS + ASK, :] = questions[start, 2 * h + kind]
            side[h, kind, 5 * ROWS + ASK :, :] = jnp.zeros((ROWS - ASK, HEAD), bf16)
    for i in range(1, 4):

        @pl.when(x + i < XS)
        def _():
            at = pl.multiple_of(jnp.minimum(x + i, XS - 1) * ROWS, ROWS)
            side[:, :, i * ROWS : (i + 1) * ROWS, :] = above[:, :, pl.ds(at, ROWS), :]

        @pl.when(x + i >= XS)
        def _():
            at = pl.multiple_of(jnp.maximum(x + i - XS, 0) * ROWS, ROWS)
            side[:, :, i * ROWS : (i + 1) * ROWS, :] = below[:, :, pl.ds(at, ROWS), :]

    i = lax.broadcasted_iota(jnp.int32, (ROWS, ROWS), 0)
    j = lax.broadcasted_iota(jnp.int32, (ROWS, ROWS), 1)
    up, down = y > start, y + 1 < stop
    first = jnp.where((y == start + 1) & (x == 0), asked, 0)
    limit = jnp.where(up, 0, ROWS)
    bias[:, 0:ROWS] = jnp.where((j >= i) & (j >= first) & (j >= limit), 0.0, MASKED)
    for b in range(1, 4):
        fine = jnp.where(x + b < XS, up.astype(jnp.int32), down.astype(jnp.int32))
        bias[:, b * ROWS : (b + 1) * ROWS] = jnp.where(j < fine * ROWS, 0.0, MASKED)
    limit = jnp.where(down, ROWS, 0)
    bias[:, 4 * ROWS : 5 * ROWS] = jnp.where((j <= i) & (j < limit), 0.0, MASKED)
    bias[:, 5 * ROWS :] = jnp.where(j < jnp.where(up, asked, 0), 0.0, MASKED)

    for n in range(KV * GROUP):
        rows[n * ROWS : (n + 1) * ROWS, :] = queries[:, head_columns(n)]
    for h in range(KV):
        q = rows[h * GROUP * ROWS : (h + 1) * GROUP * ROWS, :]
        near = lax.dot_general(q, own[h, 0], NT, preferred_element_type=f32)
        far = lax.dot_general(q, side[h, 0], NT, preferred_element_type=f32)
        far = (far.reshape(GROUP, ROWS, 6 * ROWS) + bias[...][None]).reshape(GROUP * ROWS, 6 * ROWS)
        peak = jnp.maximum(jnp.max(near, axis=1, keepdims=True), jnp.max(far, axis=1, keepdims=True))
        near = jnp.exp2((near - peak) * SCALE)
        far = jnp.exp2((far - peak) * SCALE)
        total = jnp.sum(near, axis=1, keepdims=True) + jnp.sum(far, axis=1, keepdims=True)
        sums = jnp.dot(near.astype(bf16), own[h, 1], preferred_element_type=f32)
        sums = sums + jnp.dot(far.astype(bf16), side[h, 1], preferred_element_type=f32)
        answer = (sums / total).astype(bf16)
        for g in range(GROUP):
            out[:, head_columns(GROUP * h + g)] = answer[g * ROWS : (g + 1) * ROWS]


def patch_body(tiles, lengths, banded, pack, back2, back4, out):
    y, x, start, stop, asked = place(tiles, lengths)
    out[...] = banded[...]

    @pl.when((y == start) & (x == 0))
    def _():
        chosen = lax.broadcasted_iota(jnp.int32, (ASK, HEAD), 0) < asked
        sources = ((pack, True), (back2, start + 2 < stop), (back4, start + 4 < stop))
        for h in range(KV):
            logs = []
            for source, valid in sources:
                tail = source[KV * BLOCK :, :].astype(f32)
                log = tail[3 * h : 3 * h + 1] + tail[3 * h + 1 : 3 * h + 2] + tail[3 * h + 2 : 3 * h + 3]
                logs.append(jnp.where(valid, log, MASKED))
            peak = functools.reduce(jnp.maximum, logs)
            shares = [jnp.exp2(log - peak) for log in logs]
            total = sum(shares)
            answer = jnp.zeros((BLOCK, HEAD), f32)
            for share, (source, valid) in zip(shares, sources):
                block = jnp.where(valid, source[h * BLOCK : (h + 1) * BLOCK, :].astype(f32), 0.0)
                answer = answer + to_column(share / total, BLOCK) * block
            for g in range(GROUP):
                mine = head_columns(GROUP * h + g)
                old = out[0:ASK, mine].astype(f32)
                out[0:ASK, mine] = jnp.where(chosen, answer[g * ASK : (g + 1) * ASK], old).astype(bf16)


def exchange(array, axis):
    return lax.all_to_all(array, axis, 0, 0, tiled=False)


def down(array, shift):
    return lax.ppermute(array, "y", [(y, y + shift) for y in range(YS) if 0 <= y + shift < YS])


def copies(array, n):
    return jnp.broadcast_to(array[None], (n,) + array.shape)


def along(array, shift, source, to):
    pairs = [(XS * y + source, XS * (y + shift) + to) for y in range(YS) if 0 <= y + shift < YS]
    return lax.ppermute(array, ("y", "x"), pairs)


def per_device(tokens, queries, key_matrix, value_matrix, doc_tiles, question_lengths):
    core, pair = lax.axis_index("core"), lax.axis_index("pair")
    swap = [(0, 1), (1, 0)]
    at = (doc_tiles, question_lengths)
    across = lax.ppermute(tokens, "pair", swap)

    shard = jnp.where(core == 0, key_matrix, value_matrix)
    shard = jnp.where(pair == 0, shard[:, :HEAD], shard[:, HEAD:])
    weights = exchange(copies(shard, YS * XS), ("y", "x")).reshape(tokens.shape[1], HEAD)
    head = queries[:ASK]
    sibling, corner = lax.ppermute(tokens, "core", swap), lax.ppermute(across, "core", swap)
    head2, head4 = along(head, 2, 0, 1), along(head, 4, 0, 1)
    weights, head2, head4 = lax.optimization_barrier((weights, head2, head4))

    rows = call(
        project_body, jax.ShapeDtypeStruct((2, 2, XS, ROWS, HEAD), bf16), 5, micros=2, scalars=0
    )(weights, tokens, sibling, across, corner)
    tile = exchange(rows.reshape(4 * XS, ROWS, HEAD), ("pair", "core", "x")).reshape(KV, 2, TILE, HEAD)

    above, below = down(tile, 1), down(tile, -1)
    questions = exchange(copies(tile[:, :, :ASK].reshape(2 * KV, ASK, HEAD), YS), "y")
    pack = call(
        ask_body,
        jax.ShapeDtypeStruct((PACK, HEAD), bf16),
        5,
        [pltpu.VMEM(head.shape, bf16)],
        micros=2,
    )(*at, tile, below, head, head2, head4)
    back2, back4 = along(pack, -2, 1, 0), along(pack, -4, 1, 0)

    banded = call(
        attend_body,
        jax.ShapeDtypeStruct(queries.shape, bf16),
        5,
        [
            pltpu.VMEM((KV, 2, 6 * ROWS, HEAD), bf16),
            pltpu.VMEM((ROWS, 6 * ROWS), f32),
            pltpu.VMEM((KV * GROUP * ROWS, HEAD), bf16),
        ],
        micros=5,
    )(*at, queries, tile, above, below, questions)
    top = pl.BlockSpec((ASK, queries.shape[1]), lambda i: (0, 0))
    return pl.pallas_call(
        patch_body,
        out_shape=jax.ShapeDtypeStruct(queries.shape, bf16),
        grid=(1,),
        in_specs=[spec(pltpu.SMEM)] * 2 + [top] + [spec(pltpu.VMEM)] * 3,
        out_specs=top,
        input_output_aliases={2: 0},
        compiler_params=pltpu.CompilerParams(vmem_limit_bytes=4 * 1024 * 1024),
        cost_estimate=pl.CostEstimate(flops=0, bytes_accessed=3690000, transcendentals=0),
    )(*at, banded, pack, back2, back4)


def solution(mesh):
    devices = mesh.devices
    split = Mesh(devices.reshape(devices.shape[0] // 4, 2, 2, YS, XS), ("z", "pair", "core", "y", "x"))
    rows = P(("z", "pair", "core", "y", "x"), None)
    return jax.shard_map(
        per_device,
        mesh=split,
        in_specs=(
            rows,
            rows,
            P(("y", "x"), None),
            P(("y", "x"), None),
            P(("z", "pair", "core")),
            P(("z", "pair", "core")),
        ),
        out_specs=rows,
        check_vma=False,
    )
```

```python
import functools
import math

import jax
import jax.numpy as jnp
from jax import lax
from jax.experimental import pallas as pl
from jax.experimental.pallas import tpu as pltpu
from jax.sharding import Mesh, PartitionSpec as P

HEAD = 128
TILE = 512
ASK = 16
GROUP = 7
KV = 2
ROWS = 128
XS = 4
YS = 8
BLOCK = GROUP * ASK
PACK = KV * BLOCK + 16
SCALE = math.log2(math.e) / math.sqrt(HEAD)
MASKED = -1e30
NT = (((1,), (1,)), ((), ()))
bf16, f32 = jnp.bfloat16, jnp.float32

def spec(space):
    return pl.BlockSpec(memory_space=space)


def call(body, out, ins, scratch=(), micros=1, scalars=2):
    return pl.pallas_call(
        body,
        out_shape=out,
        in_specs=[spec(pltpu.SMEM)] * scalars + [spec(pltpu.VMEM)] * ins,
        out_specs=spec(pltpu.VMEM),
        scratch_shapes=list(scratch),
        compiler_params=pltpu.CompilerParams(vmem_limit_bytes=24 * 1024 * 1024),
        cost_estimate=pl.CostEstimate(flops=0, bytes_accessed=micros * 3690000, transcendentals=0),
    )


def place(tiles, lengths):
    y, x = lax.axis_index("y"), lax.axis_index("x")
    second = y >= tiles[0]
    start = jnp.where(second, tiles[0], 0)
    stop = jnp.where(second, tiles[0] + tiles[1], tiles[0])
    return y, x, start, stop, jnp.where(second, lengths[1], lengths[0])


def project_body(weights, mine, sibling, across, corner, out):
    pair, core = lax.axis_index("pair"), lax.axis_index("core")
    for z, c, tokens in (
        (pair, core, mine),
        (pair, 1 - core, sibling),
        (1 - pair, core, across),
        (1 - pair, 1 - core, corner),
    ):
        rows = jnp.dot(tokens[...], weights[...], preferred_element_type=f32).astype(bf16)
        for x in range(XS):
            out[z, c, x] = rows


def to_row(column):
    shape = (column.shape[0], 128)
    same = lax.broadcasted_iota(jnp.int32, shape, 0) == lax.broadcasted_iota(jnp.int32, shape, 1)
    return jnp.sum(jnp.where(same, column, 0.0), axis=0, keepdims=True)


def to_column(row, n):
    shape = (n, 128)
    same = lax.broadcasted_iota(jnp.int32, shape, 0) == lax.broadcasted_iota(jnp.int32, shape, 1)
    return jnp.sum(jnp.where(same, row, 0.0), axis=1, keepdims=True)


def head_columns(n):
    return slice(n * HEAD, (n + 1) * HEAD)


def ask_body(tiles, lengths, own, below, head, head2, head4, out, asked):
    y, x, start, stop, _ = place(tiles, lengths)
    shift = y - start
    for at, source in ((2, head2), (4, head4)):

        @pl.when(shift == at)
        def _():
            asked[...] = source[...]

    @pl.when((shift != 2) & (shift != 4))
    def _():
        asked[...] = head[...]

    more = y + 1 < stop
    tail = jnp.zeros((16, 128), f32)
    line = lax.broadcasted_iota(jnp.int32, (16, 128), 0)
    for h in range(KV):
        queries = jnp.concatenate([asked[:, head_columns(GROUP * h + g)] for g in range(GROUP)], axis=0)
        near = lax.dot_general(queries, own[h, 0], NT, preferred_element_type=f32)
        far = lax.dot_general(queries, below[h, 0], NT, preferred_element_type=f32)
        far = jnp.where(more, far, MASKED)
        peak = jnp.maximum(jnp.max(near, axis=1, keepdims=True), jnp.max(far, axis=1, keepdims=True))
        sums, total = jnp.zeros((BLOCK, HEAD), f32), jnp.zeros((BLOCK, 1), f32)
        for scores, block in ((near, own), (far, below)):
            weights = jnp.exp2((scores - peak) * SCALE)
            total = total + jnp.sum(weights, axis=1, keepdims=True)
            high = weights.astype(bf16)
            low = (weights - high.astype(f32)).astype(bf16)
            sums = sums + jnp.dot(high, block[h, 1], preferred_element_type=f32)
            sums = sums + jnp.dot(low, block[h, 1], preferred_element_type=f32)
        out[h * BLOCK : (h + 1) * BLOCK, :] = (sums / total).astype(bf16)
        rest = to_row(peak * SCALE + jnp.log2(total))
        for i in range(3):
            piece = rest.astype(bf16).astype(f32)
            tail = jnp.where(line == 3 * h + i, piece, tail)
            rest = rest - piece
    out[KV * BLOCK :, :] = tail.astype(bf16)


def attend_body(
    tiles, lengths, queries, own, above, below, questions, out, side, bias, rows
):
    y, x, start, stop, asked = place(tiles, lengths)
    at = pl.multiple_of(x * ROWS, ROWS)
    side[:, :, 0:ROWS, :] = above[:, :, pl.ds(at, ROWS), :]
    side[:, :, 4 * ROWS : 5 * ROWS, :] = below[:, :, pl.ds(at, ROWS), :]
    for h in range(KV):
        for kind in range(2):
            side[h, kind, 5 * ROWS : 5 * ROWS + ASK, :] = questions[start, 2 * h + kind]
            side[h, kind, 5 * ROWS + ASK :, :] = jnp.zeros((ROWS - ASK, HEAD), bf16)
    for i in range(1, 4):

        @pl.when(x + i < XS)
        def _():
            at = pl.multiple_of(jnp.minimum(x + i, XS - 1) * ROWS, ROWS)
            side[:, :, i * ROWS : (i + 1) * ROWS, :] = above[:, :, pl.ds(at, ROWS), :]

        @pl.when(x + i >= XS)
        def _():
            at = pl.multiple_of(jnp.maximum(x + i - XS, 0) * ROWS, ROWS)
            side[:, :, i * ROWS : (i + 1) * ROWS, :] = below[:, :, pl.ds(at, ROWS), :]

    i = lax.broadcasted_iota(jnp.int32, (ROWS, ROWS), 0)
    j = lax.broadcasted_iota(jnp.int32, (ROWS, ROWS), 1)
    up, down = y > start, y + 1 < stop
    first = jnp.where((y == start + 1) & (x == 0), asked, 0)
    limit = jnp.where(up, 0, ROWS)
    bias[:, 0:ROWS] = jnp.where((j >= i) & (j >= first) & (j >= limit), 0.0, MASKED)
    for b in range(1, 4):
        fine = jnp.where(x + b < XS, up.astype(jnp.int32), down.astype(jnp.int32))
        bias[:, b * ROWS : (b + 1) * ROWS] = jnp.where(j < fine * ROWS, 0.0, MASKED)
    limit = jnp.where(down, ROWS, 0)
    bias[:, 4 * ROWS : 5 * ROWS] = jnp.where((j <= i) & (j < limit), 0.0, MASKED)
    bias[:, 5 * ROWS :] = jnp.where(j < jnp.where(up, asked, 0), 0.0, MASKED)

    for n in range(KV * GROUP):
        rows[n * ROWS : (n + 1) * ROWS, :] = queries[:, head_columns(n)]
    for h in range(KV):
        q = rows[h * GROUP * ROWS : (h + 1) * GROUP * ROWS, :]
        near = lax.dot_general(q, own[h, 0], NT, preferred_element_type=f32)
        far = lax.dot_general(q, side[h, 0], NT, preferred_element_type=f32)
        far = (far.reshape(GROUP, ROWS, 6 * ROWS) + bias[...][None]).reshape(GROUP * ROWS, 6 * ROWS)
        peak = jnp.maximum(jnp.max(near, axis=1, keepdims=True), jnp.max(far, axis=1, keepdims=True))
        near = jnp.exp2((near - peak) * SCALE)
        far = jnp.exp2((far - peak) * SCALE)
        total = jnp.sum(near, axis=1, keepdims=True) + jnp.sum(far, axis=1, keepdims=True)
        sums = jnp.dot(near.astype(bf16), own[h, 1], preferred_element_type=f32)
        sums = sums + jnp.dot(far.astype(bf16), side[h, 1], preferred_element_type=f32)
        answer = (sums / total).astype(bf16)
        for g in range(GROUP):
            out[:, head_columns(GROUP * h + g)] = answer[g * ROWS : (g + 1) * ROWS]


def patch_body(tiles, lengths, banded, pack, back2, back4, out, top, arrived, left):
    y, x, start, stop, asked = place(tiles, lengths)

    @pl.when((y == start) & (x == 0))
    def _():
        fetch = pltpu.make_async_copy(banded.at[pl.ds(0, ASK), :], top, arrived)
        fetch.start()
        chosen = lax.broadcasted_iota(jnp.int32, (ASK, HEAD), 0) < asked
        sources = ((pack, True), (back2, start + 2 < stop), (back4, start + 4 < stop))
        answers = []
        for h in range(KV):
            logs = []
            for source, valid in sources:
                tail = source[KV * BLOCK :, :].astype(f32)
                log = tail[3 * h : 3 * h + 1] + tail[3 * h + 1 : 3 * h + 2] + tail[3 * h + 2 : 3 * h + 3]
                logs.append(jnp.where(valid, log, MASKED))
            peak = functools.reduce(jnp.maximum, logs)
            shares = [jnp.exp2(log - peak) for log in logs]
            total = sum(shares)
            answer = jnp.zeros((BLOCK, HEAD), f32)
            for share, (source, valid) in zip(shares, sources):
                block = jnp.where(valid, source[h * BLOCK : (h + 1) * BLOCK, :].astype(f32), 0.0)
                answer = answer + to_column(share / total, BLOCK) * block
            answers.append(answer)
        fetch.wait()
        for h in range(KV):
            for g in range(GROUP):
                mine = head_columns(GROUP * h + g)
                old = top[:, mine].astype(f32)
                top[:, mine] = jnp.where(chosen, answers[h][g * ASK : (g + 1) * ASK], old).astype(bf16)
        store = pltpu.make_async_copy(top, out.at[pl.ds(0, ASK), :], left)
        store.start()
        store.wait()


def exchange(array, axis):
    return lax.all_to_all(array, axis, 0, 0, tiled=False)


def down(array, shift):
    return lax.ppermute(array, "y", [(y, y + shift) for y in range(YS) if 0 <= y + shift < YS])


def copies(array, n):
    return jnp.broadcast_to(array[None], (n,) + array.shape)


def along(array, shift, source, to):
    pairs = [(XS * y + source, XS * (y + shift) + to) for y in range(YS) if 0 <= y + shift < YS]
    return lax.ppermute(array, ("y", "x"), pairs)


def per_device(tokens, queries, key_matrix, value_matrix, doc_tiles, question_lengths):
    core, pair = lax.axis_index("core"), lax.axis_index("pair")
    swap = [(0, 1), (1, 0)]
    at = (doc_tiles, question_lengths)
    across = lax.ppermute(tokens, "pair", swap)

    shard = jnp.where(core == 0, key_matrix, value_matrix)
    shard = jnp.where(pair == 0, shard[:, :HEAD], shard[:, HEAD:])
    weights = exchange(copies(shard, YS * XS), ("y", "x")).reshape(tokens.shape[1], HEAD)
    head = queries[:ASK]
    sibling, corner = lax.ppermute(tokens, "core", swap), lax.ppermute(across, "core", swap)
    head2, head4 = along(head, 2, 0, 1), along(head, 4, 0, 1)
    weights, head2, head4 = lax.optimization_barrier((weights, head2, head4))

    rows = call(
        project_body, jax.ShapeDtypeStruct((2, 2, XS, ROWS, HEAD), bf16), 5, micros=2, scalars=0
    )(weights, tokens, sibling, across, corner)
    tile = exchange(rows.reshape(4 * XS, ROWS, HEAD), ("pair", "core", "x")).reshape(KV, 2, TILE, HEAD)

    above, below = down(tile, 1), down(tile, -1)
    questions = exchange(copies(tile[:, :, :ASK].reshape(2 * KV, ASK, HEAD), YS), "y")
    pack = call(
        ask_body,
        jax.ShapeDtypeStruct((PACK, HEAD), bf16),
        5,
        [pltpu.VMEM(head.shape, bf16)],
        micros=2,
    )(*at, tile, below, head, head2, head4)
    back2, back4 = along(pack, -2, 1, 0), along(pack, -4, 1, 0)

    banded = call(
        attend_body,
        jax.ShapeDtypeStruct(queries.shape, bf16),
        5,
        [
            pltpu.VMEM((KV, 2, 6 * ROWS, HEAD), bf16),
            pltpu.VMEM((ROWS, 6 * ROWS), f32),
            pltpu.VMEM((KV * GROUP * ROWS, HEAD), bf16),
        ],
        micros=5,
    )(*at, queries, tile, above, below, questions)
    return pl.pallas_call(
        patch_body,
        out_shape=jax.ShapeDtypeStruct(queries.shape, bf16),
        in_specs=[spec(pltpu.SMEM)] * 2 + [spec(pl.ANY)] + [spec(pltpu.VMEM)] * 3,
        out_specs=spec(pl.ANY),
        scratch_shapes=[
            pltpu.VMEM((ASK, queries.shape[1]), bf16),
            pltpu.SemaphoreType.DMA,
            pltpu.SemaphoreType.DMA,
        ],
        input_output_aliases={2: 0},
        compiler_params=pltpu.CompilerParams(vmem_limit_bytes=4 * 1024 * 1024),
        cost_estimate=pl.CostEstimate(flops=0, bytes_accessed=3690000, transcendentals=0),
    )(*at, banded, pack, back2, back4)


def solution(mesh):
    devices = mesh.devices
    split = Mesh(devices.reshape(devices.shape[0] // 4, 2, 2, YS, XS), ("z", "pair", "core", "y", "x"))
    rows = P(("z", "pair", "core", "y", "x"), None)
    return jax.shard_map(
        per_device,
        mesh=split,
        in_specs=(
            rows,
            rows,
            P(("y", "x"), None),
            P(("y", "x"), None),
            P(("z", "pair", "core")),
            P(("z", "pair", "core")),
        ),
        out_specs=rows,
        check_vma=False,
    )
```

```python
import functools
import math

import jax
import jax.numpy as jnp
from jax import lax
from jax.experimental import pallas as pl
from jax.experimental.pallas import tpu as pltpu
from jax.sharding import Mesh, PartitionSpec as P

HEAD = 128
TILE = 512
ASK = 16
GROUP = 7
KV = 2
ROWS = 128
XS = 4
YS = 8
BLOCK = GROUP * ASK
PACK = KV * BLOCK + 16
SCALE = math.log2(math.e) / math.sqrt(HEAD)
MASKED = -1e30
NT = (((1,), (1,)), ((), ()))
bf16, f32 = jnp.bfloat16, jnp.float32

def spec(space):
    return pl.BlockSpec(memory_space=space)


def call(body, out, ins, scratch=(), micros=1, scalars=2):
    return pl.pallas_call(
        body,
        out_shape=out,
        in_specs=[spec(pltpu.SMEM)] * scalars + [spec(pltpu.VMEM)] * ins,
        out_specs=spec(pltpu.VMEM),
        scratch_shapes=list(scratch),
        compiler_params=pltpu.CompilerParams(vmem_limit_bytes=24 * 1024 * 1024),
        cost_estimate=pl.CostEstimate(flops=0, bytes_accessed=micros * 3690000, transcendentals=0),
    )


def place(tiles, lengths):
    y, x = lax.axis_index("y"), lax.axis_index("x")
    second = y >= tiles[0]
    start = jnp.where(second, tiles[0], 0)
    stop = jnp.where(second, tiles[0] + tiles[1], tiles[0])
    return y, x, start, stop, jnp.where(second, lengths[1], lengths[0])


def project_body(weights, mine, sibling, across, corner, out, whole):
    depth = weights.shape[2]
    for x in range(XS):
        for y in range(YS):
            whole[pl.ds((XS * y + x) * depth, depth), :] = weights[x, y]
    pair, core = lax.axis_index("pair"), lax.axis_index("core")
    for z, c, tokens in (
        (pair, core, mine),
        (pair, 1 - core, sibling),
        (1 - pair, core, across),
        (1 - pair, 1 - core, corner),
    ):
        rows = jnp.dot(tokens[...], whole[...], preferred_element_type=f32).astype(bf16)
        for x in range(XS):
            out[z, c, x] = rows


def to_row(column):
    shape = (column.shape[0], 128)
    same = lax.broadcasted_iota(jnp.int32, shape, 0) == lax.broadcasted_iota(jnp.int32, shape, 1)
    return jnp.sum(jnp.where(same, column, 0.0), axis=0, keepdims=True)


def to_column(row, n):
    shape = (n, 128)
    same = lax.broadcasted_iota(jnp.int32, shape, 0) == lax.broadcasted_iota(jnp.int32, shape, 1)
    return jnp.sum(jnp.where(same, row, 0.0), axis=1, keepdims=True)


def head_columns(n):
    return slice(n * HEAD, (n + 1) * HEAD)


def ask_body(tiles, lengths, own, below, head, head2, head4, out, asked):
    y, x, start, stop, _ = place(tiles, lengths)
    shift = y - start
    for at, source in ((2, head2), (4, head4)):

        @pl.when(shift == at)
        def _():
            asked[...] = source[...]

    @pl.when((shift != 2) & (shift != 4))
    def _():
        asked[...] = head[...]

    more = y + 1 < stop
    tail = jnp.zeros((16, 128), f32)
    line = lax.broadcasted_iota(jnp.int32, (16, 128), 0)
    for h in range(KV):
        queries = jnp.concatenate([asked[:, head_columns(GROUP * h + g)] for g in range(GROUP)], axis=0)
        near = lax.dot_general(queries, own[h, 0], NT, preferred_element_type=f32)
        far = lax.dot_general(queries, below[h, 0], NT, preferred_element_type=f32)
        far = jnp.where(more, far, MASKED)
        peak = jnp.maximum(jnp.max(near, axis=1, keepdims=True), jnp.max(far, axis=1, keepdims=True))
        sums, total = jnp.zeros((BLOCK, HEAD), f32), jnp.zeros((BLOCK, 1), f32)
        for scores, block in ((near, own), (far, below)):
            weights = jnp.exp2((scores - peak) * SCALE)
            total = total + jnp.sum(weights, axis=1, keepdims=True)
            high = weights.astype(bf16)
            low = (weights - high.astype(f32)).astype(bf16)
            sums = sums + jnp.dot(high, block[h, 1], preferred_element_type=f32)
            sums = sums + jnp.dot(low, block[h, 1], preferred_element_type=f32)
        out[h * BLOCK : (h + 1) * BLOCK, :] = (sums / total).astype(bf16)
        rest = to_row(peak * SCALE + jnp.log2(total))
        for i in range(3):
            piece = rest.astype(bf16).astype(f32)
            tail = jnp.where(line == 3 * h + i, piece, tail)
            rest = rest - piece
    out[KV * BLOCK :, :] = tail.astype(bf16)


def attend_body(
    tiles, lengths, queries, own, above, below, questions, out, side, bias, rows
):
    y, x, start, stop, asked = place(tiles, lengths)
    at = pl.multiple_of(x * ROWS, ROWS)
    side[:, :, 0:ROWS, :] = above[:, :, pl.ds(at, ROWS), :]
    side[:, :, 4 * ROWS : 5 * ROWS, :] = below[:, :, pl.ds(at, ROWS), :]
    for h in range(KV):
        for kind in range(2):
            side[h, kind, 5 * ROWS : 5 * ROWS + ASK, :] = questions[start, 2 * h + kind]
            side[h, kind, 5 * ROWS + ASK :, :] = jnp.zeros((ROWS - ASK, HEAD), bf16)
    for i in range(1, 4):

        @pl.when(x + i < XS)
        def _():
            at = pl.multiple_of(jnp.minimum(x + i, XS - 1) * ROWS, ROWS)
            side[:, :, i * ROWS : (i + 1) * ROWS, :] = above[:, :, pl.ds(at, ROWS), :]

        @pl.when(x + i >= XS)
        def _():
            at = pl.multiple_of(jnp.maximum(x + i - XS, 0) * ROWS, ROWS)
            side[:, :, i * ROWS : (i + 1) * ROWS, :] = below[:, :, pl.ds(at, ROWS), :]

    i = lax.broadcasted_iota(jnp.int32, (ROWS, ROWS), 0)
    j = lax.broadcasted_iota(jnp.int32, (ROWS, ROWS), 1)
    up, down = y > start, y + 1 < stop
    first = jnp.where((y == start + 1) & (x == 0), asked, 0)
    limit = jnp.where(up, 0, ROWS)
    bias[:, 0:ROWS] = jnp.where((j >= i) & (j >= first) & (j >= limit), 0.0, MASKED)
    for b in range(1, 4):
        fine = jnp.where(x + b < XS, up.astype(jnp.int32), down.astype(jnp.int32))
        bias[:, b * ROWS : (b + 1) * ROWS] = jnp.where(j < fine * ROWS, 0.0, MASKED)
    limit = jnp.where(down, ROWS, 0)
    bias[:, 4 * ROWS : 5 * ROWS] = jnp.where((j <= i) & (j < limit), 0.0, MASKED)
    bias[:, 5 * ROWS :] = jnp.where(j < jnp.where(up, asked, 0), 0.0, MASKED)

    for n in range(KV * GROUP):
        rows[n * ROWS : (n + 1) * ROWS, :] = queries[:, head_columns(n)]
    for h in range(KV):
        q = rows[h * GROUP * ROWS : (h + 1) * GROUP * ROWS, :]
        near = lax.dot_general(q, own[h, 0], NT, preferred_element_type=f32)
        far = lax.dot_general(q, side[h, 0], NT, preferred_element_type=f32)
        far = (far.reshape(GROUP, ROWS, 6 * ROWS) + bias[...][None]).reshape(GROUP * ROWS, 6 * ROWS)
        peak = jnp.maximum(jnp.max(near, axis=1, keepdims=True), jnp.max(far, axis=1, keepdims=True))
        near = jnp.exp2((near - peak) * SCALE)
        far = jnp.exp2((far - peak) * SCALE)
        total = jnp.sum(near, axis=1, keepdims=True) + jnp.sum(far, axis=1, keepdims=True)
        sums = jnp.dot(near.astype(bf16), own[h, 1], preferred_element_type=f32)
        sums = sums + jnp.dot(far.astype(bf16), side[h, 1], preferred_element_type=f32)
        answer = (sums / total).astype(bf16)
        for g in range(GROUP):
            out[:, head_columns(GROUP * h + g)] = answer[g * ROWS : (g + 1) * ROWS]


def patch_body(tiles, lengths, banded, pack, back2, back4, out, top, arrived, left):
    y, x, start, stop, asked = place(tiles, lengths)

    @pl.when((y == start) & (x == 0))
    def _():
        fetch = pltpu.make_async_copy(banded.at[pl.ds(0, ASK), :], top, arrived)
        fetch.start()
        chosen = lax.broadcasted_iota(jnp.int32, (ASK, HEAD), 0) < asked
        sources = ((pack, True), (back2, start + 2 < stop), (back4, start + 4 < stop))
        answers = []
        for h in range(KV):
            logs = []
            for source, valid in sources:
                tail = source[KV * BLOCK :, :].astype(f32)
                log = tail[3 * h : 3 * h + 1] + tail[3 * h + 1 : 3 * h + 2] + tail[3 * h + 2 : 3 * h + 3]
                logs.append(jnp.where(valid, log, MASKED))
            peak = functools.reduce(jnp.maximum, logs)
            shares = [jnp.exp2(log - peak) for log in logs]
            total = sum(shares)
            answer = jnp.zeros((BLOCK, HEAD), f32)
            for share, (source, valid) in zip(shares, sources):
                block = jnp.where(valid, source[h * BLOCK : (h + 1) * BLOCK, :].astype(f32), 0.0)
                answer = answer + to_column(share / total, BLOCK) * block
            answers.append(answer)
        fetch.wait()
        for h in range(KV):
            for g in range(GROUP):
                mine = head_columns(GROUP * h + g)
                old = top[:, mine].astype(f32)
                top[:, mine] = jnp.where(chosen, answers[h][g * ASK : (g + 1) * ASK], old).astype(bf16)
        store = pltpu.make_async_copy(top, out.at[pl.ds(0, ASK), :], left)
        store.start()
        store.wait()


def exchange(array, axis):
    return lax.all_to_all(array, axis, 0, 0, tiled=False)


def down(array, shift):
    return lax.ppermute(array, "y", [(y, y + shift) for y in range(YS) if 0 <= y + shift < YS])


def copies(array, n):
    return jnp.broadcast_to(array[None], (n,) + array.shape)


def along(array, shift, source, to):
    pairs = [(XS * y + source, XS * (y + shift) + to) for y in range(YS) if 0 <= y + shift < YS]
    return lax.ppermute(array, ("y", "x"), pairs)


def per_device(tokens, queries, key_matrix, value_matrix, doc_tiles, question_lengths):
    core, pair = lax.axis_index("core"), lax.axis_index("pair")
    swap = [(0, 1), (1, 0)]
    at = (doc_tiles, question_lengths)
    across = lax.ppermute(tokens, "pair", swap)

    shard = jnp.where(core == 0, key_matrix, value_matrix)
    shard = jnp.where(pair == 0, shard[:, :HEAD], shard[:, HEAD:])
    weights = exchange(copies(shard, YS * XS), ("x", "y"))
    weights = weights.reshape((XS, YS) + weights.shape[1:])
    head = queries[:ASK]
    sibling, corner = lax.ppermute(tokens, "core", swap), lax.ppermute(across, "core", swap)
    head2, head4 = along(head, 2, 0, 1), along(head, 4, 0, 1)
    weights, head2, head4 = lax.optimization_barrier((weights, head2, head4))

    rows = call(
        project_body,
        jax.ShapeDtypeStruct((2, 2, XS, ROWS, HEAD), bf16),
        5,
        [pltpu.VMEM((tokens.shape[1], HEAD), bf16)],
        micros=2,
        scalars=0,
    )(weights, tokens, sibling, across, corner)
    tile = exchange(rows.reshape(4 * XS, ROWS, HEAD), ("pair", "core", "x")).reshape(KV, 2, TILE, HEAD)

    above, below = down(tile, 1), down(tile, -1)
    questions = exchange(copies(tile[:, :, :ASK].reshape(2 * KV, ASK, HEAD), YS), "y")
    pack = call(
        ask_body,
        jax.ShapeDtypeStruct((PACK, HEAD), bf16),
        5,
        [pltpu.VMEM(head.shape, bf16)],
        micros=2,
    )(*at, tile, below, head, head2, head4)
    back2, back4 = along(pack, -2, 1, 0), along(pack, -4, 1, 0)

    banded = call(
        attend_body,
        jax.ShapeDtypeStruct(queries.shape, bf16),
        5,
        [
            pltpu.VMEM((KV, 2, 6 * ROWS, HEAD), bf16),
            pltpu.VMEM((ROWS, 6 * ROWS), f32),
            pltpu.VMEM((KV * GROUP * ROWS, HEAD), bf16),
        ],
        micros=5,
    )(*at, queries, tile, above, below, questions)
    return pl.pallas_call(
        patch_body,
        out_shape=jax.ShapeDtypeStruct(queries.shape, bf16),
        in_specs=[spec(pltpu.SMEM)] * 2 + [spec(pl.ANY)] + [spec(pltpu.VMEM)] * 3,
        out_specs=spec(pl.ANY),
        scratch_shapes=[
            pltpu.VMEM((ASK, queries.shape[1]), bf16),
            pltpu.SemaphoreType.DMA,
            pltpu.SemaphoreType.DMA,
        ],
        input_output_aliases={2: 0},
        compiler_params=pltpu.CompilerParams(vmem_limit_bytes=4 * 1024 * 1024),
        cost_estimate=pl.CostEstimate(flops=0, bytes_accessed=3690000, transcendentals=0),
    )(*at, banded, pack, back2, back4)


def solution(mesh):
    devices = mesh.devices
    split = Mesh(devices.reshape(devices.shape[0] // 4, 2, 2, YS, XS), ("z", "pair", "core", "y", "x"))
    rows = P(("z", "pair", "core", "y", "x"), None)
    return jax.shard_map(
        per_device,
        mesh=split,
        in_specs=(
            rows,
            rows,
            P(("y", "x"), None),
            P(("y", "x"), None),
            P(("z", "pair", "core")),
            P(("z", "pair", "core")),
        ),
        out_specs=rows,
        check_vma=False,
    )
```
